128 devices in a mesh: region: 4 (over x), shard: 32 (over z, y, core).
Axes of the slice: x: 4, y: 4, z: 4, core: 2. Of those that a mesh axis runs over, the one named last changes fastest.
Arguments:
- features: bfloat16 [128, 512, 256], P(('region', 'shard')), may hold values from -6 to 6
- cotangent: bfloat16 [128, 512, 256], P(('region', 'shard')), may hold values from -6 to 6
- weight_one: bfloat16 [27, 256, 256], replicated, may hold values from -0.078125 to 0.078125
- weight_two: bfloat16 [27, 256, 256], replicated, may hold values from -0.078125 to 0.078125
- occupancy: int32 [128], P(('region', 'shard')), may hold values from 0 to 1, as said below
- neighbour_owner: int32 [128, 26], P(('region', 'shard')), may hold values from -1 to 127, as said below
- neighbour_slot: int32 [128, 26], P(('region', 'shard')), may hold values from -1 to 0, as said below
Outputs:
- output: bfloat16 [128, 512, 256], P(('region', 'shard'))
- grad_input: bfloat16 [128, 512, 256], P(('region', 'shard'))
- grad_weight_one: bfloat16 [27, 256, 256], replicated
- grad_weight_two: bfloat16 [27, 256, 256], replicated
The draws below stay inside these ranges and needn't reach their ends.
Inputs may be any that keep to these rules, and one draw needn't show every extreme that they name: `occupancy`: live bricks fill the first slots of a device; a device may hold none; the first three and the last three devices have all 1 slots live. `neighbour_owner`: for each brick and offset, the device (numbered region-major) holding the neighbouring brick, or -1 where there is none. Neighbours lie on the same device or on a device at most two places earlier or later in that numbering, and two places is reached. Adjacency is symmetric: if brick b has neighbour n at offset o, then n has b at offset -o. Only live bricks have neighbours, and every neighbour is live. `neighbour_slot`: the neighbour's slot on its device, -1 exactly where neighbour_owner is -1.
All inputs are finite; a program needn't handle non-finite values.
Results may differ from the reference program's by a relative error of at most 0.0053.
Values may be sent and summed in bfloat16 or wider, within the bound.
No kernel may reach another device: no remote copies, remote signals or barrier semaphores. Data moves between devices by JAX's collectives and lax.ppermute only.
A program may use at most 128 MiB of HBM per device.

```python
import jax
import jax.numpy as jnp
from jax import lax

CHANNELS = 256
BRICK_EDGE = 8
SLOTS = 1
BRICKS = 128


def brick_graph(key):
    device_count = BRICKS // SLOTS
    occupancy_key, full_key, stride_key, coin_key = jax.random.split(key, 4)
    occupancy = jax.random.randint(occupancy_key, (device_count,), 0, SLOTS + 1).astype(jnp.int32)
    full_device = jax.random.randint(full_key, (), 0, device_count)
    device_ids = jnp.arange(device_count)
    always_full = (device_ids == full_device) | (device_ids < 3) | (device_ids >= device_count - 3)
    occupancy = jnp.where(always_full, SLOTS, occupancy).astype(jnp.int32)
    strides = jax.random.randint(stride_key, (13,), 1, 2 * SLOTS + 1)
    strides = strides.at[0].set(2 * SLOTS).at[1].set(SLOTS)
    brick_ids = jnp.arange(BRICKS)
    live_mask = brick_ids % SLOTS < occupancy[brick_ids // SLOTS]
    coins = jax.random.randint(coin_key, (BRICKS, 13), 0, 5) > 0
    coins = coins.at[:, 0].set(True)
    ahead = brick_ids[:, None] + strides[None, :]
    ahead_safe = jnp.clip(ahead, 0, BRICKS - 1)
    ahead_ok = (ahead < BRICKS) & live_mask[:, None] & live_mask[ahead_safe] & coins
    behind = brick_ids[:, None] - strides[None, :]
    behind_safe = jnp.clip(behind, 0, BRICKS - 1)
    behind_coins = coins[behind_safe, jnp.arange(13)[None, :]]
    behind_ok = (behind >= 0) & live_mask[:, None] & live_mask[behind_safe] & behind_coins
    forward_ids = jnp.where(ahead_ok, ahead, -1)
    backward_ids = jnp.where(behind_ok, behind, -1)[:, ::-1]
    neighbour = jnp.concatenate([forward_ids, backward_ids], axis=1).astype(jnp.int32)
    return (occupancy, neighbour)


def draw_occupancy(key, part):
    occupancy, neighbour = brick_graph(key)
    return occupancy


def draw_neighbour_owner(key, part):
    occupancy, neighbour = brick_graph(key)
    return jnp.where(neighbour >= 0, neighbour // SLOTS, -1).astype(jnp.int32)


def draw_neighbour_slot(key, part):
    occupancy, neighbour = brick_graph(key)
    return jnp.where(neighbour >= 0, neighbour % SLOTS, -1).astype(jnp.int32)


def levels(key, dims, cuts, low, high):
    gain, own = 1.0, jax.random.fold_in(key, 6)
    for dim, shards_of in cuts:
        heights = jnp.exp(jax.random.uniform(jax.random.fold_in(own, dim), (shards_of,), jnp.float32, low / len(cuts), high / len(cuts)))
        gain = gain * jnp.repeat(heights, dims[dim] // shards_of).reshape([-1 if axis == dim else 1 for axis in range(len(dims))])
    return gain


def normal_values(key, shape, spread, most, cuts=(), kind=jnp.bfloat16):
    entries = spread * jax.random.normal(key, shape, jnp.float32)
    if cuts:
        entries = entries * levels(key, shape, cuts, -0.22, 0.18)
    return jnp.clip(entries, -most, most).astype(kind)


def setup_inputs(seed: int = 0) -> dict:
    key_list = jax.random.split(jax.random.key(seed), 8)
    return {
        "features": normal_values(key_list[0], (BRICKS, BRICK_EDGE ** 3, CHANNELS), 1.0, 6.0, ((0, 128),)),
        "cotangent": normal_values(key_list[1], (BRICKS, BRICK_EDGE ** 3, CHANNELS), 1.0, 6.0, ((0, 128),)),
        "weight_one": normal_values(key_list[2], (27, CHANNELS, CHANNELS), (27 * CHANNELS) ** -0.5, 0.078125),
        "weight_two": normal_values(key_list[3], (27, CHANNELS, CHANNELS), (27 * CHANNELS) ** -0.5, 0.078125),
        "occupancy": draw_occupancy(jax.random.fold_in(key_list[7], 71), 0),
        "neighbour_owner": draw_neighbour_owner(jax.random.fold_in(key_list[7], 71), 0),
        "neighbour_slot": draw_neighbour_slot(jax.random.fold_in(key_list[7], 71), 0),
    }


every_offset = [(step_x, step_y, step_z) for step_x in (-1, 0, 1) for step_y in (-1, 0, 1) for step_z in (-1, 0, 1)]
reversed_offset = every_offset[::-1]
side_offsets = [entry for entry in every_offset if entry != (0, 0, 0)]


def source_range(direction):
    if direction > 0:
        return slice(0, 1)
    if direction < 0:
        return slice(BRICK_EDGE - 1, BRICK_EDGE)
    return slice(0, BRICK_EDGE)


def target_range(direction):
    if direction > 0:
        return slice(BRICK_EDGE + 1, BRICK_EDGE + 2)
    if direction < 0:
        return slice(0, 1)
    return slice(1, BRICK_EDGE + 1)


def framed(centre, sources, picked, present):
    channels = centre.shape[-1]
    edge_cells = BRICK_EDGE
    framed_grid = jnp.zeros((edge_cells + 2, edge_cells + 2, edge_cells + 2, channels), centre.dtype)
    framed_grid = framed_grid.at[1:edge_cells + 1, 1:edge_cells + 1, 1:edge_cells + 1].set(
        centre.reshape(edge_cells, edge_cells, edge_cells, channels))
    for position, (step_x, step_y, step_z) in enumerate(side_offsets):
        source = lax.dynamic_index_in_dim(sources, picked[position], 0, keepdims=False)
        source = source.reshape(edge_cells, edge_cells, edge_cells, channels)
        pieces = source[source_range(step_x), source_range(step_y), source_range(step_z)]
        pieces = jnp.where(present[position], pieces, jnp.zeros_like(pieces))
        framed_grid = framed_grid.at[target_range(step_x), target_range(step_y), target_range(step_z)].set(pieces)
    return framed_grid


def unfolded(framed_grid, offsets):
    edge_cells = BRICK_EDGE
    channels = framed_grid.shape[-1]
    patches = []
    for step_x, step_y, step_z in offsets:
        window = framed_grid[1 + step_x:1 + step_x + edge_cells, 1 + step_y:1 + step_y + edge_cells,
                             1 + step_z:1 + step_z + edge_cells]
        patches.append(window.reshape(edge_cells ** 3, channels))
    return jnp.concatenate(patches, axis=1)


def convolve_all(field_data, flat_weights, offsets, picked, present):
    def one_brick(brick_id):
        framed_grid = framed(field_data[brick_id], field_data, picked[brick_id], present[brick_id])
        return jnp.dot(unfolded(framed_grid, offsets), flat_weights, preferred_element_type=jnp.float32)
    return lax.map(one_brick, jnp.arange(BRICKS, dtype=jnp.int32))


def reference(features, cotangent, weight_one, weight_two, occupancy, neighbour_owner, neighbour_slot):
    channels = features.shape[-1]
    brick_ids = jnp.arange(BRICKS, dtype=jnp.int32)
    live_mask = ((brick_ids % SLOTS) < occupancy[brick_ids // SLOTS])[:, None, None]
    present = neighbour_owner >= 0
    picked = jnp.where(present, neighbour_owner * SLOTS + neighbour_slot, 0).astype(jnp.int32)
    masked_in = jnp.where(live_mask, features, jnp.zeros_like(features))
    masked_cot = jnp.where(live_mask, cotangent, jnp.zeros_like(cotangent))
    flat_one = weight_one.reshape(27 * channels, channels)
    flat_two = weight_two.reshape(27 * channels, channels)
    turned_one = jnp.transpose(weight_one, (0, 2, 1)).reshape(27 * channels, channels)
    turned_two = jnp.transpose(weight_two, (0, 2, 1)).reshape(27 * channels, channels)
    pre_act = convolve_all(masked_in, flat_one, every_offset, picked, present)
    hidden = jax.nn.silu(pre_act).astype(jnp.bfloat16)
    output = convolve_all(hidden, flat_two, every_offset, picked, present).astype(jnp.bfloat16)
    grad_hidden = convolve_all(masked_cot, turned_two, reversed_offset, picked, present)
    sigmoid_pre = jax.nn.sigmoid(pre_act)
    grad_pre = (grad_hidden * sigmoid_pre * (1.0 + pre_act * (1.0 - sigmoid_pre))).astype(jnp.bfloat16)
    grad_input = convolve_all(grad_pre, turned_one, reversed_offset, picked, present).astype(jnp.bfloat16)

    def accumulate(carry, brick_id):
        total_one, total_two = carry
        grid_in = framed(masked_in[brick_id], masked_in, picked[brick_id], present[brick_id])
        grid_hidden = framed(hidden[brick_id], hidden, picked[brick_id], present[brick_id])
        total_two = total_two + jnp.dot(unfolded(grid_hidden, every_offset).T, masked_cot[brick_id],
                                        preferred_element_type=jnp.float32)
        total_one = total_one + jnp.dot(unfolded(grid_in, every_offset).T, grad_pre[brick_id],
                                        preferred_element_type=jnp.float32)
        return (total_one, total_two), None

    empty = jnp.zeros((27 * channels, channels), jnp.float32)
    (total_one, total_two), unused = lax.scan(accumulate, (empty, empty), brick_ids)
    grad_scale = float(BRICKS * BRICK_EDGE ** 3) ** -0.5
    grad_weight_one = (grad_scale * total_one).astype(jnp.bfloat16).reshape(27, channels, channels)
    grad_weight_two = (grad_scale * total_two).astype(jnp.bfloat16).reshape(27, channels, channels)
    return output, grad_input, grad_weight_one, grad_weight_two
```

```python
import jax
import jax.numpy as jnp
from jax import lax
from jax.experimental import pallas as pl
from jax.experimental.pallas import tpu as pltpu
from jax.sharding import PartitionSpec as P

AXES = ("region", "shard")
SIDES = (4, 4, 4, 2)
ROWS = 512
CH = 256
TAPS = 2304
FRAME_ROWS = 640
F32 = jnp.float32
BF16 = jnp.bfloat16
VMEM_LIMIT = 40 * 1024 * 1024
VMEM_SPEC = pl.BlockSpec(memory_space=pltpu.VMEM)
SMEM_SPEC = pl.BlockSpec(memory_space=pltpu.SMEM)
ANY_SPEC = pl.BlockSpec(memory_space=pl.ANY)


def coordinates(index):
    return {"x": index // 32, "z": (index // 8) % 4, "y": (index // 2) % 4, "core": index % 2}


def device_at(place):
    return place["x"] * 32 + place["z"] * 8 + place["y"] * 2 + place["core"]


def ring_send(array, axis_of_core, step):
    pairs = []
    for index in range(128):
        place = coordinates(index)
        axis = axis_of_core[place["core"]]
        place[axis] = (place[axis] + step) % 4
        pairs.append((index, device_at(place)))
    return lax.ppermute(array, AXES, pairs)


def swap(array):
    return lax.ppermute(array, AXES, [(index, index ^ 1) for index in range(128)])


def shifted(array, by):
    return lax.ppermute(array, AXES, [(i, i + by) for i in range(128) if 0 <= i + by < 128])


def build(stack, field, pick, out, first_row):
    z_of = lax.broadcasted_iota(jnp.int32, (10, 8, CH), 1)

    def plane(X, sx, xp):
        base = pl.multiple_of(xp * 64, 64)

        def column(sz):
            low = stack[field, pick(sx, 0, sz), pl.ds(base + 48, 16), :].astype(F32)[8:16]
            mid = stack[field, pick(sx, 1, sz), pl.ds(base, 64), :].astype(F32)
            high = stack[field, pick(sx, 2, sz), pl.ds(base, 16), :].astype(F32)[0:8]
            return jnp.concatenate([low, mid, high], axis=0).reshape(10, 8, CH)

        below, here, above = column(0), column(1), column(2)
        shifts = (
            pltpu.roll(jnp.where(z_of == 7, below, here), 1, 1),
            here,
            pltpu.roll(jnp.where(z_of == 0, above, here), 7, 1),
        )
        rows = pl.ds(pl.multiple_of(first_row + X * 64, 64), 64)
        for dz, grid in enumerate(shifts):
            even = grid.reshape(80, CH).astype(BF16)
            odd = grid[1:9].reshape(64, CH).astype(BF16)
            out[rows, (0 + dz) * CH : (1 + dz) * CH] = even[0:64]
            out[rows, (3 + dz) * CH : (4 + dz) * CH] = odd
            out[rows, (6 + dz) * CH : (7 + dz) * CH] = even[16:80]

    plane(0, 0, 7)

    @pl.loop(1, 9)
    def _(X):
        plane(X, 1, X - 1)

    plane(9, 2, 0)


def convolved(frame, weights):
    total = jnp.dot(frame[0:ROWS, :], weights[0], preferred_element_type=F32)
    total += jnp.dot(frame[64 : 64 + ROWS, :], weights[1], preferred_element_type=F32)
    total += jnp.dot(frame[128 : 128 + ROWS, :], weights[2], preferred_element_type=F32)
    return total


def load_stack(bricks, stack, sems):
    copies = [
        pltpu.make_async_copy(brick, stack.at[:, place], sems.at[place])
        for place, brick in enumerate(bricks)
    ]
    for copy in copies:
        copy.start()
    stack[:, 6] = jnp.zeros((2, ROWS, CH), BF16)
    for copy in copies:
        copy.wait()


def first_kernel(
    pick_ref, core_ref, own, before, after, mate, mate_before, mate_after, weight_one, turned_two,
    hidden_grad, frames, stack, spare, sems
):
    load_stack((own, before, after, mate, mate_before, mate_after), stack, sems)
    core = core_ref[0]

    def pick_of(which):
        return lambda sx, sy, sz: pick_ref[which, 9 * sx + 3 * sy + sz]

    build(stack, 1 - core, pick_of(0), frames, 0)
    build(stack, core, pick_of(0), spare, 0)
    build(stack, 1 - core, pick_of(1), frames, FRAME_ROWS)

    def finish(frame_in, frame_cot):
        pre_act = convolved(frame_in, weight_one)
        grad_hidden = convolved(frame_cot, turned_two)
        sig = 1.0 / (1.0 + jnp.exp(-pre_act))
        hidden_grad[0] = (pre_act * sig).astype(BF16)
        hidden_grad[1] = (grad_hidden * sig * (1.0 + pre_act * (1.0 - sig))).astype(BF16)

    @pl.when(core == 0)
    def _():
        finish(spare, frames)

    @pl.when(core != 0)
    def _():
        finish(frames, spare)


def second_kernel(
    pick_ref, own, before, after, mate, mate_before, mate_after, weight_two, turned_one,
    output, grad_input, stack, frame, sems
):
    load_stack((own, before, after, mate, mate_before, mate_after), stack, sems)

    def pick(sx, sy, sz):
        return pick_ref[0, 9 * sx + 3 * sy + sz]

    build(stack, 0, pick, frame, 0)
    output[...] = convolved(frame, weight_two).astype(BF16)
    build(stack, 1, pick, frame, 0)
    grad_input[...] = convolved(frame, turned_one).astype(BF16)


def gradient_kernel(place_ref, own, mate, frames, *rest):
    parts_a, parts_b, (turned, block) = rest[0:4], rest[4:8], rest[8:]
    core = place_ref[0]
    turned[0] = own[core].astype(F32).T.astype(BF16)
    turned[1] = mate[core].astype(F32).T.astype(BF16)

    def one(k, parts, axis_place, first):
        window = jnp.where(core == 0, 26 - k, k)
        row = pl.multiple_of((window // 9) * 64, 64)
        lane = pl.multiple_of((window % 9) * CH, CH)
        total = jnp.dot(turned[0], frames[pl.ds(row, ROWS), pl.ds(lane, CH)], preferred_element_type=F32)
        total += jnp.dot(
            turned[1], frames[pl.ds(FRAME_ROWS + row, ROWS), pl.ds(lane, CH)], preferred_element_type=F32
        )

        @pl.when(core == 0)
        def _():
            block[...] = total

        @pl.when(core != 0)
        def _():
            block[...] = total.T

        for step in range(4):
            chunk = pl.multiple_of(((axis_place + step) % 4) * 64, 64)
            parts[step][k - first] = block[pl.ds(chunk, 64), :].astype(BF16)

    @pl.loop(0, 18)
    def _(k):
        one(k, parts_a, place_ref[1], 0)

    @pl.loop(18, 27)
    def _(k):
        one(k, parts_b, place_ref[2], 18)


def scatter_kernel(place_ref, *refs):
    ins_a, ins_b, outs = refs[0:4], refs[4:8], refs[8:12]
    for step in range(4):
        rows = pl.ds(pl.multiple_of(((place_ref[3] + step) % 4) * 16, 16), 16)
        for ins, first, count in ((ins_a, 0, 18), (ins_b, 18, 9)):
            total = (ins[0][:, rows, :].astype(F32) + ins[2][:, rows, :].astype(F32)) + (
                ins[1][:, rows, :].astype(F32) + ins[3][:, rows, :].astype(F32)
            )
            outs[step][first : first + count] = total.astype(BF16)


def gather_kernel(place_ref, part0, part1, part2, part3, out_a, out_b):
    for step, part in enumerate((part0, part1, part2, part3)):
        rows = pl.ds(pl.multiple_of(((place_ref[3] + 4 - step) % 4) * 16, 16), 16)
        out_a[:, rows, :] = part[0:18]
        out_b[:, rows, :] = part[18:27]


def final_kernel(place_ref, *refs):
    own_a, own_b, mate_a, mate_b = refs[0:4], refs[4:8], refs[8:12], refs[12:16]
    grad_one, grad_two, sems = refs[16:]
    core = place_ref[0]

    def copies(dst, parts_a, parts_b, place_a, place_b, sem):
        made = []
        for step in range(4):
            rows_a = pl.ds(pl.multiple_of(((place_a + 4 - step) % 4) * 64, 64), 64)
            rows_b = pl.ds(pl.multiple_of(((place_b + 4 - step) % 4) * 64, 64), 64)
            made.append(pltpu.make_async_copy(parts_a[step], dst.at[0:18, rows_a, :], sem.at[step]))
            made.append(pltpu.make_async_copy(parts_b[step], dst.at[18:27, rows_b, :], sem.at[4 + step]))
        return made

    def run(one, two):
        made = copies(one[0], one[1], one[2], one[3], place_ref[2], sems.at[0])
        made += copies(two[0], two[1], two[2], two[3], place_ref[2], sems.at[1])
        for copy in made:
            copy.start()
        for copy in made:
            copy.wait()

    @pl.when(core == 0)
    def _():
        run((grad_two, own_a, own_b, place_ref[1]), (grad_one, mate_a, mate_b, place_ref[3]))

    @pl.when(core != 0)
    def _():
        run((grad_one, own_a, own_b, place_ref[1]), (grad_two, mate_a, mate_b, place_ref[3]))


def call(kernel, name, outs, in_specs, out_specs, scratch, flops, moved):
    return pl.pallas_call(
        kernel,
        name=name,
        out_shape=[jax.ShapeDtypeStruct(shape, BF16) for shape in outs],
        in_specs=in_specs,
        out_specs=out_specs,
        scratch_shapes=scratch,
        compiler_params=pltpu.CompilerParams(vmem_limit_bytes=VMEM_LIMIT),
        cost_estimate=pl.CostEstimate(flops=flops, bytes_accessed=moved, transcendentals=0),
    )


def on_device(
    features, cotangent, weight_one, weight_two, occupancy, neighbour_owner, neighbour_slot
):
    index = lax.axis_index(AXES)
    here = coordinates(index)
    core = here["core"]
    first_axis = jnp.where(core == 0, here["x"], here["z"])
    second_axis = jnp.where(core == 0, here["z"], here["x"])
    place = jnp.stack([core, first_axis, here["y"], second_axis]).astype(jnp.int32)

    graph = jnp.concatenate([occupancy.reshape(1, 1), neighbour_owner], axis=1)
    graph_mate = swap(graph)
    two = jnp.concatenate([graph, graph_mate], axis=0)
    first_brick = index - core - 2
    own_brick = jnp.stack([index, index ^ 1])[:, None]
    own_brick = jnp.where(two[:, 0:1] > 0, own_brick, -1)
    owners = jnp.concatenate([two[:, 1:14], own_brick, two[:, 14:27]], axis=1)
    rel = owners - first_brick
    same = (rel % 2) == core
    kind = jnp.where(rel // 2 == 1, 0, jnp.where(rel // 2 == 0, 1, 2))
    picks = jnp.where(owners >= 0, jnp.where(same, kind, kind + 3), 6).astype(jnp.int32)

    one = weight_one.reshape(3, TAPS, CH)
    two_w = weight_two.reshape(3, TAPS, CH)
    turned_one = jnp.transpose(weight_one[::-1], (0, 2, 1)).reshape(3, TAPS, CH)
    turned_two = jnp.transpose(weight_two[::-1], (0, 2, 1)).reshape(3, TAPS, CH)

    def halo(field):
        before, after = shifted(field, 2), shifted(field, -2)
        return field, before, after, swap(field), swap(before), swap(after)

    stack = pltpu.VMEM((2, 7, ROWS, CH), BF16)
    sems = pltpu.SemaphoreType.DMA((6,))
    fields = jnp.concatenate([features, cotangent], axis=0)
    hidden_grad, frames = call(
        first_kernel, "first_convs",
        [(2, ROWS, CH), (2 * FRAME_ROWS, TAPS)],
        [SMEM_SPEC, SMEM_SPEC] + [ANY_SPEC] * 6 + [VMEM_SPEC] * 2, [VMEM_SPEC] * 2,
        [stack, pltpu.VMEM((FRAME_ROWS, TAPS), BF16), sems],
        4 * ROWS * TAPS * 3 * CH, 16_000_000,
    )(picks, place, *halo(fields), one, turned_two)

    hidden_grad_mate = swap(hidden_grad)
    parts = call(
        gradient_kernel, "weight_grads",
        [(18, 64, CH)] * 4 + [(9, 64, CH)] * 4,
        [SMEM_SPEC] + [VMEM_SPEC] * 3, [VMEM_SPEC] * 8,
        [pltpu.VMEM((2, CH, ROWS), BF16), pltpu.VMEM((CH, CH), F32)],
        4 * ROWS * TAPS * 3 * CH, 10_000_000,
    )(place, hidden_grad, hidden_grad_mate, frames)
    parts_a, parts_b = parts[0:4], parts[4:8]

    axis_a, axis_b, axis_c = ("x", "z"), ("y", "y"), ("z", "x")
    sent_a = [parts_a[0]] + [ring_send(parts_a[d], axis_a, d) for d in (1, 2, 3)]
    sent_b = [parts_b[0]] + [ring_send(parts_b[d], axis_b, d) for d in (1, 2, 3)]
    quarter = call(
        scatter_kernel, "sum_and_split", [(27, 16, CH)] * 4,
        [SMEM_SPEC] + [VMEM_SPEC] * 8, [VMEM_SPEC] * 4, [], 4_000_000, 4_500_000,
    )(place, *sent_a, *sent_b)
    sent = [quarter[0]] + [ring_send(quarter[d], axis_c, d) for d in (1, 2, 3)]

    def added(arrays):
        wide = [array.astype(F32) for array in arrays]
        return (wide[0] + wide[2]) + (wide[1] + wide[3])

    small = added(sent).astype(BF16)
    small_a, small_b = small[0:18], small[18:27]
    all_a = added([small_a] + [ring_send(small_a, axis_b, d) for d in (1, 2, 3)])
    all_b = added([small_b] + [ring_send(small_b, axis_a, d) for d in (1, 2, 3)])
    scale = float(128 * ROWS) ** (-0.5)
    whole = (scale * jnp.concatenate([all_a, all_b], axis=0)).astype(BF16)

    back = [whole] + [ring_send(whole, axis_c, d) for d in (1, 2, 3)]
    wide_a, wide_b = call(
        gather_kernel, "gather_rows", [(18, 64, CH), (9, 64, CH)],
        [SMEM_SPEC] + [VMEM_SPEC] * 4, [VMEM_SPEC] * 2, [], 1000, 1_800_000,
    )(place, *back)
    final_a = [wide_a] + [ring_send(wide_a, axis_a, d) for d in (1, 2, 3)]
    final_b = [wide_b] + [ring_send(wide_b, axis_b, d) for d in (1, 2, 3)]
    mate_a = [swap(array) for array in final_a]
    mate_b = [swap(array) for array in final_b]
    grad_one, grad_two = call(
        final_kernel, "place_rows", [(27, CH, CH)] * 2,
        [SMEM_SPEC] + [VMEM_SPEC] * 16, [ANY_SPEC] * 2,
        [pltpu.SemaphoreType.DMA((2, 8))], 1000, 14_000_000,
    )(place, *final_a, *final_b, *mate_a, *mate_b)

    before, after = shifted(hidden_grad, 2), shifted(hidden_grad, -2)
    output, grad_input = call(
        second_kernel, "second_convs",
        [(ROWS, CH)] * 2,
        [SMEM_SPEC] + [ANY_SPEC] * 6 + [VMEM_SPEC] * 2, [VMEM_SPEC] * 2,
        [stack, pltpu.VMEM((FRAME_ROWS, TAPS), BF16), sems],
        4 * ROWS * TAPS * 3 * CH, 12_000_000,
    )(picks, hidden_grad, before, after, hidden_grad_mate, swap(before), swap(after), two_w, turned_one)

    return output[None], grad_input[None], grad_one, grad_two


def solution(mesh):
    by_brick = P(AXES, None, None)
    in_specs = (by_brick, by_brick, P(), P(), P(AXES), P(AXES, None), P(AXES, None))
    out_specs = (by_brick, by_brick, P(), P())
    return jax.shard_map(
        on_device, mesh=mesh, in_specs=in_specs, out_specs=out_specs, check_vma=False
    )
```

```python
import jax
import jax.numpy as jnp
from jax import lax
from jax.experimental import pallas as pl
from jax.experimental.pallas import tpu as pltpu
from jax.sharding import PartitionSpec as P

AXES = ("region", "shard")
SIDES = (4, 4, 4, 2)
ROWS = 512
CH = 256
TAPS = 2304
FRAME_ROWS = 640
F32 = jnp.float32
BF16 = jnp.bfloat16
VMEM_SPEC = pl.BlockSpec(memory_space=pltpu.VMEM)
SMEM_SPEC = pl.BlockSpec(memory_space=pltpu.SMEM)
ANY_SPEC = pl.BlockSpec(memory_space=pl.ANY)
HBM_SPEC = pl.BlockSpec(memory_space=pltpu.HBM)


def coordinates(index):
    return {"x": index // 32, "z": (index // 8) % 4, "y": (index // 2) % 4, "core": index % 2}


def device_at(place):
    return place["x"] * 32 + place["z"] * 8 + place["y"] * 2 + place["core"]


def ring_send(array, axis_of_core, step):
    pairs = []
    for index in range(128):
        place = coordinates(index)
        axis = axis_of_core[place["core"]]
        place[axis] = (place[axis] + step) % 4
        pairs.append((index, device_at(place)))
    return lax.ppermute(array, AXES, pairs)


def swap(array):
    return lax.ppermute(array, AXES, [(index, index ^ 1) for index in range(128)])


def shifted(array, by):
    return lax.ppermute(array, AXES, [(i, i + by) for i in range(128) if 0 <= i + by < 128])


def build(stack, field, pick, out, first_row):
    z_of = lax.broadcasted_iota(jnp.int32, (10, 8, CH), 1)

    def plane(X, sx, xp):
        base = pl.multiple_of(xp * 64, 64)

        def column(sz):
            low = stack[field, pick(sx, 0, sz), pl.ds(base + 48, 16), :].astype(F32)[8:16]
            mid = stack[field, pick(sx, 1, sz), pl.ds(base, 64), :].astype(F32)
            high = stack[field, pick(sx, 2, sz), pl.ds(base, 16), :].astype(F32)[0:8]
            return jnp.concatenate([low, mid, high], axis=0).reshape(10, 8, CH)

        below, here, above = column(0), column(1), column(2)
        shifts = (
            pltpu.roll(jnp.where(z_of == 7, below, here), 1, 1),
            here,
            pltpu.roll(jnp.where(z_of == 0, above, here), 7, 1),
        )
        rows = pl.ds(pl.multiple_of(first_row + X * 64, 64), 64)
        for dz, grid in enumerate(shifts):
            even = grid.reshape(80, CH).astype(BF16)
            odd = grid[1:9].reshape(64, CH).astype(BF16)
            out[rows, (0 + dz) * CH : (1 + dz) * CH] = even[0:64]
            out[rows, (3 + dz) * CH : (4 + dz) * CH] = odd
            out[rows, (6 + dz) * CH : (7 + dz) * CH] = even[16:80]

    plane(0, 0, 7)

    @pl.loop(1, 9)
    def _(X):
        plane(X, 1, X - 1)

    plane(9, 2, 0)


def convolved(frame, weights):
    total = None
    for plane in range(3):
        term = jnp.dot(
            frame[64 * plane : 64 * plane + ROWS, :],
            weights[9 * plane : 9 * plane + 9].reshape(TAPS, CH),
            preferred_element_type=F32,
        )
        total = term if total is None else total + term
    return total


def convolved_turned(frame, weights):
    total = None
    for k in range(27):
        window = frame[64 * (k // 9) : 64 * (k // 9) + ROWS, (k % 9) * CH : (k % 9 + 1) * CH]
        term = lax.dot_general(
            window, weights[26 - k], (((1,), (1,)), ((), ())), preferred_element_type=F32
        )
        total = term if total is None else total + term
    return total


def picker(pick_ref, which):
    return lambda sx, sy, sz: pick_ref[which, 9 * sx + 3 * sy + sz]


def loaded(bricks, weights, stack, held, sems):
    copies = [
        pltpu.make_async_copy(brick, stack.at[:, place], sems.at[place])
        for place, brick in enumerate(bricks)
    ]
    loads = [
        pltpu.make_async_copy(weight, held.at[place], sems.at[6 + place])
        for place, weight in enumerate(weights)
    ]
    for copy in copies + loads:
        copy.start()
    stack[:, 6] = jnp.zeros((2, ROWS, CH), BF16)
    for copy in copies:
        copy.wait()
    return loads


def order_kernel(passed, waited_for, passed_out):
    pass


def pack_kernel(features, cotangent, out, sems):
    copies = [
        pltpu.make_async_copy(field.at[0], out.at[place], sems.at[place])
        for place, field in enumerate((features, cotangent))
    ]
    for copy in copies:
        copy.start()
    for copy in copies:
        copy.wait()


def frames_kernel(
    pick_ref, place_ref, own, before, after, mate, mate_before, mate_after, frames, spare, stack, sems
):
    loaded((own, before, after, mate, mate_before, mate_after), (), stack, None, sems)
    core = place_ref[0]
    build(stack, 1 - core, picker(pick_ref, 0), frames, 0)
    build(stack, core, picker(pick_ref, 0), spare, 0)
    build(stack, 1 - core, picker(pick_ref, 1), frames, FRAME_ROWS)


def hidden_kernel(place_ref, frames, spare, weight_one, pre_act):
    @pl.when(place_ref[0] == 0)
    def _():
        pre_act[...] = convolved(spare, weight_one)

    @pl.when(place_ref[0] != 0)
    def _():
        pre_act[...] = convolved(frames, weight_one)


def grad_kernel(place_ref, frames, spare, weight_two, pre_act_ref, both):
    def finish(frame):
        grad_hidden = convolved_turned(frame, weight_two)
        pre_act = pre_act_ref[...]
        sig = 1.0 / (1.0 + jnp.exp(-pre_act))
        both[0] = (pre_act / (1.0 + jnp.exp(-pre_act))).astype(BF16)
        both[1] = (grad_hidden * sig * (1.0 + pre_act * (1.0 - sig))).astype(BF16)

    @pl.when(place_ref[0] == 0)
    def _():
        finish(frames)

    @pl.when(place_ref[0] != 0)
    def _():
        finish(spare)


def outer_kernel(
    pick_ref, own, before, after, mate, mate_before, mate_after, weight_two, weight_one, passed,
    output, grad_input, passed_out, frame, stack, held, sems
):
    bricks = (own, before, after, mate, mate_before, mate_after)
    loads = loaded(bricks, (weight_two, weight_one), stack, held, sems)
    build(stack, 0, picker(pick_ref, 0), frame, 0)
    loads[0].wait()
    output[0] = convolved(frame, held.at[0]).astype(BF16)
    build(stack, 1, picker(pick_ref, 0), frame, 0)
    loads[1].wait()
    grad_input[0] = convolved_turned(frame, held.at[1]).astype(BF16)


def gradient_kernel(place_ref, both, both_mate, frames, passed, *rest):
    parts, (turned, blocks) = rest[0:4], rest[5:]
    core = place_ref[0]
    turned[0] = both[core].T
    turned[1] = both_mate[core].T

    def run(core):
        for plane in range(3):
            for third in range(3):
                lanes = slice(third * 3 * CH, (third + 1) * 3 * CH)
                row = 64 * plane
                total = jnp.dot(turned[0], frames[row : row + ROWS, lanes], preferred_element_type=F32)
                row += FRAME_ROWS
                total += jnp.dot(turned[1], frames[row : row + ROWS, lanes], preferred_element_type=F32)
                for tap in range(3):
                    k = 9 * plane + 3 * third + tap
                    block = total[:, tap * CH : (tap + 1) * CH].astype(BF16)
                    if core == 0:
                        blocks[26 - k] = block
                    else:
                        blocks[k] = block.T

    @pl.when(core == 0)
    def _():
        run(0)

    @pl.when(core != 0)
    def _():
        run(1)

    for step in range(4):
        rows = pl.ds(pl.multiple_of(((place_ref[1] + step) % 4) * 64, 64), 64)
        parts[step][...] = blocks[:, rows, :]


def scatter_kernel(place_ref, *refs):
    ins, outs = refs[0:4], refs[4:8]
    for step in range(4):
        rows = pl.ds(pl.multiple_of(((place_ref[3] + step) % 4) * 16, 16), 16)
        total = (ins[0][:, rows, :].astype(F32) + ins[2][:, rows, :].astype(F32)) + (
            ins[1][:, rows, :].astype(F32) + ins[3][:, rows, :].astype(F32)
        )
        outs[step][...] = total.astype(BF16)


def gather_kernel(place_ref, part0, part1, part2, part3, passed, wide, again, passed_out):
    for step, part in enumerate((part0, part1, part2, part3)):
        rows = pl.ds(pl.multiple_of(((place_ref[3] + 4 - step) % 4) * 16, 16), 16)
        wide[:, rows, :] = part[...]
        again[:, rows, :] = part[...]


def final_kernel(place_ref, *refs):
    own, mate = refs[0:4], refs[4:8]
    grad_one, grad_two, sems = refs[8:]

    def copies(dst, parts, place, sem):
        return [
            pltpu.make_async_copy(
                parts[step],
                dst.at[:, pl.ds(pl.multiple_of(((place + 4 - step) % 4) * 64, 64), 64), :],
                sem.at[step],
            )
            for step in range(4)
        ]

    def run(own_dst, mate_dst):
        made = copies(own_dst, own, place_ref[1], sems.at[0])
        made += copies(mate_dst, mate, place_ref[2], sems.at[1])
        for copy in made:
            copy.start()
        for copy in made:
            copy.wait()

    @pl.when(place_ref[0] == 0)
    def _():
        run(grad_two, grad_one)

    @pl.when(place_ref[0] != 0)
    def _():
        run(grad_one, grad_two)


def call(kernel, name, outs, in_specs, out_specs, scratch, flops, moved, mib, aliases=None):
    return pl.pallas_call(
        kernel,
        name=name,
        out_shape=[
            jax.ShapeDtypeStruct(*out) if isinstance(out[0], tuple) else jax.ShapeDtypeStruct(out, BF16)
            for out in outs
        ],
        in_specs=in_specs,
        out_specs=out_specs,
        scratch_shapes=scratch,
        input_output_aliases=aliases or {},
        compiler_params=pltpu.CompilerParams(vmem_limit_bytes=mib * 1024 * 1024),
        cost_estimate=pl.CostEstimate(flops=flops, bytes_accessed=moved, transcendentals=0),
    )


def on_device(
    features, cotangent, weight_one, weight_two, occupancy, neighbour_owner, neighbour_slot
):
    index = lax.axis_index(AXES)
    here = coordinates(index)
    core = here["core"]
    first, second, third = ("x", "z"), ("z", "y"), ("y", "x")

    def along(axis, which):
        return jnp.where(which == 0, here[axis[0]], here[axis[1]])

    place = jnp.stack([core, along(first, core), along(first, 1 - core), along(second, core)])
    place = place.astype(jnp.int32)

    graph = jnp.concatenate([occupancy.reshape(1, 1), neighbour_owner], axis=1)
    graph_mate = swap(graph)
    two = jnp.concatenate([graph, graph_mate], axis=0)
    first_brick = index - core - 2
    own_brick = jnp.stack([index, index ^ 1])[:, None]
    own_brick = jnp.where(two[:, 0:1] > 0, own_brick, -1)
    owners = jnp.concatenate([two[:, 1:14], own_brick, two[:, 14:27]], axis=1)
    rel = owners - first_brick
    same = (rel % 2) == core
    kind = jnp.where(rel // 2 == 1, 0, jnp.where(rel // 2 == 0, 1, 2))
    picks = jnp.where(owners >= 0, jnp.where(same, kind, kind + 3), 6).astype(jnp.int32)

    def sent_halo(field):
        return shifted(field, 2), shifted(field, -2)

    flops = 2 * ROWS * TAPS * 3 * CH
    stack = pltpu.VMEM((2, 7, ROWS, CH), BF16)
    frame = pltpu.VMEM((FRAME_ROWS, TAPS), BF16)
    held = pltpu.VMEM((2, 27, CH, CH), BF16)
    sems = pltpu.SemaphoreType.DMA((8,))
    pair = (2, ROWS, CH)
    rows64, rows16 = (27, 64, CH), (27, 16, CH)

    (fields,) = call(
        pack_kernel, "pack_fields", [pair], [HBM_SPEC] * 2, [VMEM_SPEC],
        [pltpu.SemaphoreType.DMA((2,))], 1000, 1_000_000, 60,
    )(features, cotangent)
    before, after = sent_halo(fields)
    frames, spare = call(
        frames_kernel, "build_frames", [(2 * FRAME_ROWS, TAPS), (FRAME_ROWS, TAPS)],
        [SMEM_SPEC] * 2 + [ANY_SPEC] * 6, [VMEM_SPEC] * 2, [stack, sems], 1_000_000, 12_000_000, 14,
    )(picks, place, fields, before, after, swap(fields), swap(before), swap(after))
    (pre_act,) = call(
        hidden_kernel, "first_conv", [((ROWS, CH), F32)], [SMEM_SPEC] + [VMEM_SPEC] * 3, [VMEM_SPEC], [],
        flops, 4_000_000, 14,
    )(place, frames, spare, weight_one)
    (both,) = call(
        grad_kernel, "grad_conv", [pair], [SMEM_SPEC] + [VMEM_SPEC] * 4, [VMEM_SPEC], [],
        flops, 4_000_000, 14,
    )(place, frames, spare, weight_two, pre_act)
    both_mate = swap(both)

    *parts, both = call(
        gradient_kernel, "weight_grads", [rows64] * 4 + [pair],
        [SMEM_SPEC] + [VMEM_SPEC] * 3 + [ANY_SPEC], [VMEM_SPEC] * 4 + [ANY_SPEC],
        [pltpu.VMEM((2, CH, ROWS), BF16), pltpu.VMEM((27, CH, CH), BF16)],
        2 * flops, 10_000_000, 18, {4: 4},
    )(place, both, both_mate, frames, both)

    def rounds(arrays, axis):
        return [arrays[0]] + [ring_send(arrays[d], axis, d) for d in (1, 2, 3)]

    arrived = rounds(parts, first)
    quarter = call(
        scatter_kernel, "sum_and_split", [rows16] * 4, [SMEM_SPEC] + [VMEM_SPEC] * 4, [VMEM_SPEC] * 4,
        [], 4_000_000, 4_500_000, 12,
    )(place, *arrived)

    (both,) = call(
        order_kernel, "after_first_arrival", [pair], [ANY_SPEC] * 2, [ANY_SPEC], [], 1000, 1000, 8, {0: 0},
    )(both, quarter[0])
    before, after = sent_halo(both)
    mate_before, mate_after = swap(before), swap(after)
    def added(arrays):
        wide = [array.astype(F32) for array in arrays]
        return (wide[0] + wide[2]) + (wide[1] + wide[3])

    small = added(rounds(quarter, second)).astype(BF16)
    scale = float(128 * ROWS) ** (-0.5)
    whole = (scale * added(rounds([small] * 4, third))).astype(BF16)

    wide, again, both = call(
        gather_kernel, "gather_rows", [rows64] * 2 + [pair],
        [SMEM_SPEC] + [VMEM_SPEC] * 4 + [ANY_SPEC], [VMEM_SPEC] * 2 + [ANY_SPEC], [],
        1000, 2_700_000, 12, {5: 2},
    )(place, *rounds([whole] * 4, second), both)
    chunks = rounds([wide] * 4, first)
    output, grad_input, again = call(
        outer_kernel, "outer_convs", [(1, ROWS, CH)] * 2 + [rows64],
        [SMEM_SPEC] + [ANY_SPEC] * 6 + [HBM_SPEC] * 2 + [ANY_SPEC], [VMEM_SPEC] * 2 + [ANY_SPEC],
        [frame, stack, held, sems],
        2 * flops, 12_000_000, 18, {9: 2},
    )(picks, both, before, after, both_mate, mate_before, mate_after, weight_two, weight_one, again)
    mates = [swap(again)] + [swap(chunk) for chunk in chunks[1:]]
    grad_one, grad_two = call(
        final_kernel, "place_rows", [(27, CH, CH)] * 2,
        [SMEM_SPEC] + [VMEM_SPEC] * 8, [ANY_SPEC] * 2,
        [pltpu.SemaphoreType.DMA((2, 4))], 1000, 14_000_000, 12,
    )(place, *chunks, *mates)
    return output, grad_input, grad_one, grad_two


def solution(mesh):
    by_brick = P(AXES, None, None)
    in_specs = (by_brick, by_brick, P(), P(), P(AXES), P(AXES, None), P(AXES, None))
    out_specs = (by_brick, by_brick, P(), P())
    return jax.shard_map(
        on_device, mesh=mesh, in_specs=in_specs, out_specs=out_specs, check_vma=False
    )
```

```python
from functools import partial

import jax
import jax.numpy as jnp
from jax import lax
from jax.experimental import pallas as pl
from jax.experimental.pallas import tpu as pltpu
from jax.sharding import PartitionSpec as P

AXES = ("region", "shard")
SIDES = (4, 4, 4, 2)
ROWS = 512
OUTER = 320
CH = 256
TAPS = 2304
FRAME_ROWS = 640
EVEN = (1, 0, 3, 2)
ODD = (3, 2, 1, 0)
F32 = jnp.float32
BF16 = jnp.bfloat16
VMEM_SPEC = pl.BlockSpec(memory_space=pltpu.VMEM)
SMEM_SPEC = pl.BlockSpec(memory_space=pltpu.SMEM)
ANY_SPEC = pl.BlockSpec(memory_space=pl.ANY)
HBM_SPEC = pl.BlockSpec(memory_space=pltpu.HBM)


def coordinates(index):
    return {"x": index // 32, "z": (index // 8) % 4, "y": (index // 2) % 4, "core": index % 2}


def device_at(place):
    return place["x"] * 32 + place["z"] * 8 + place["y"] * 2 + place["core"]


def ring_send(array, axis_of_core, step, pairing=(None, None)):
    pairs = []
    for index in range(128):
        place = coordinates(index)
        axis = axis_of_core[place["core"]]
        place[axis] = (place[axis] + step) % 4
        partner = pairing[place["core"]]
        place["y"] = partner[place["y"]] if partner else place["y"]
        pairs.append((index, device_at(place)))
    return lax.ppermute(array, AXES, pairs)


def swap(array):
    return lax.ppermute(array, AXES, [(index, index ^ 1) for index in range(128)])


def shifted(array, by):
    return lax.ppermute(array, AXES, [(i, i + by) for i in range(128) if 0 <= i + by < 128])


def pack(brick, packed, field):
    packed[field, 0:64] = brick[0:64]
    packed[field, 64:128] = brick[448:512]
    for x in range(1, 7):
        slab = brick[64 * x : 64 * x + 64].astype(F32).reshape(8, 8, CH)
        edges = jnp.concatenate([slab[0], slab[7], slab[:, 0, :], slab[:, 7, :]], axis=0)
        packed[field, 96 + 32 * x : 128 + 32 * x] = edges.astype(BF16)


def build(full, packed, field, pick, out, first_row):
    z_of = lax.broadcasted_iota(jnp.int32, (10, 8, CH), 1)
    centre = pick(1, 1, 1) // 3

    def outer(sx, sy, sz, first, count):
        return packed[field, pick(sx, sy, sz), pl.ds(first, count), :].astype(F32)

    def plane(X, columns):
        below, here, above = [
            jnp.concatenate([low[None], mid, high[None]], axis=0) for low, mid, high in columns
        ]
        shifts = (
            pltpu.roll(jnp.where(z_of == 7, below, here), 1, 1),
            here,
            pltpu.roll(jnp.where(z_of == 0, above, here), 7, 1),
        )
        rows = pl.ds(pl.multiple_of(first_row + X * 64, 64), 64)
        for dz, grid in enumerate(shifts):
            even = grid.reshape(80, CH).astype(BF16)
            odd = grid[1:9].reshape(64, CH).astype(BF16)
            out[rows, (0 + dz) * CH : (1 + dz) * CH] = even[0:64]
            out[rows, (3 + dz) * CH : (4 + dz) * CH] = odd
            out[rows, (6 + dz) * CH : (7 + dz) * CH] = even[16:80]

    def inside(xp):
        return full[field, centre, pl.ds(pl.multiple_of(xp * 64, 64), 64), :].astype(F32).reshape(8, 8, CH)

    for X, sx, face in ((0, 0, 64), (1, 1, 0), (8, 1, 64), (9, 2, 0)):
        columns = []
        for sz in range(3):
            if sx == 1 and sz == 1:
                mid = inside(X - 1)
            else:
                mid = outer(sx, 1, sz, face, 64).reshape(8, 8, CH)
            columns.append((outer(sx, 0, sz, face + 48, 16)[8:16], mid, outer(sx, 2, sz, face, 16)[0:8]))
        plane(X, columns)

    @pl.loop(2, 8)
    def _(X):
        first = pl.multiple_of(64 + 32 * X, 32)
        columns = []
        for sz in range(3):
            if sz == 1:
                mid = inside(X - 1)
            else:
                edge = outer(1, 1, sz, first + 16, 16)
                edge = edge[8:16] if sz == 0 else edge[0:8]
                mid = jnp.broadcast_to(edge[:, None, :], (8, 8, CH))
            columns.append((outer(1, 0, sz, first, 16)[8:16], mid, outer(1, 2, sz, first, 16)[0:8]))
        plane(X, columns)


def convolved(frame, weights):
    total = None
    for plane in range(3):
        term = jnp.dot(
            frame[64 * plane : 64 * plane + ROWS, :],
            weights[9 * plane : 9 * plane + 9].reshape(TAPS, CH),
            preferred_element_type=F32,
        )
        total = term if total is None else total + term
    return total


def convolved_turned(frame, weights):
    total = None
    for k in range(27):
        window = frame[64 * (k // 9) : 64 * (k // 9) + ROWS, (k % 9) * CH : (k % 9 + 1) * CH]
        term = lax.dot_general(
            window, weights[26 - k], (((1,), (1,)), ((), ())), preferred_element_type=F32
        )
        total = term if total is None else total + term
    return total


def picker(pick_ref, which):
    return lambda sx, sy, sz: pick_ref[which, 9 * sx + 3 * sy + sz]


def loaded(own, mate, outers, weights, full, packed, held, sems):
    copies = [
        pltpu.make_async_copy(brick, full.at[:, place], sems.at[place])
        for place, brick in enumerate((own, mate))
    ]
    copies += [
        pltpu.make_async_copy(brick, packed.at[:, place], sems.at[2 + place])
        for place, brick in enumerate(outers)
    ]
    loads = [
        pltpu.make_async_copy(weight, held.at[place], sems.at[8 + place])
        for place, weight in enumerate(weights)
    ]
    for copy in copies + loads:
        copy.start()
    full[:, 2] = jnp.zeros((2, ROWS, CH), BF16)
    packed[:, 6] = jnp.zeros((2, OUTER, CH), BF16)
    for copy in copies:
        copy.wait()
    return loads


def order_kernel(passed, waited_for, passed_out):
    pass


def pack_kernel(features, cotangent, out, packed):
    for place, field in enumerate((features, cotangent)):
        out[place] = field[0]
        pack(field.at[0], packed, place)


def pack_both_kernel(both, waited_for, packed):
    for place in range(2):
        pack(both.at[place], packed, place)


def frames_kernel(
    pick_ref, place_ref, own, mate, packed_own, before, after, packed_mate, mate_before, mate_after,
    frames, spare, full, packed, sems
):
    outers = (packed_own, before, after, packed_mate, mate_before, mate_after)
    loaded(own, mate, outers, (), full, packed, None, sems)
    core = place_ref[0]
    build(full, packed, 1 - core, picker(pick_ref, 0), frames, 0)
    build(full, packed, core, picker(pick_ref, 0), spare, 0)
    build(full, packed, 1 - core, picker(pick_ref, 1), frames, FRAME_ROWS)


def hidden_kernel(place_ref, frames, spare, weight_one, pre_act):
    @pl.when(place_ref[0] == 0)
    def _():
        pre_act[...] = convolved(spare, weight_one)

    @pl.when(place_ref[0] != 0)
    def _():
        pre_act[...] = convolved(frames, weight_one)


def grad_kernel(place_ref, frames, spare, weight_two, pre_act_ref, both):
    def finish(frame):
        grad_hidden = convolved_turned(frame, weight_two)
        pre_act = pre_act_ref[...]
        sig = 1.0 / (1.0 + jnp.exp(-pre_act))
        both[0] = (pre_act / (1.0 + jnp.exp(-pre_act))).astype(BF16)
        both[1] = (grad_hidden * sig * (1.0 + pre_act * (1.0 - sig))).astype(BF16)

    @pl.when(place_ref[0] == 0)
    def _():
        finish(frames)

    @pl.when(place_ref[0] != 0)
    def _():
        finish(spare)


def outer_kernel(
    pick_ref, own, mate, packed_own, before, after, packed_mate, mate_before, mate_after,
    weight_two, weight_one, passed, output, grad_input, passed_out, frame, full, packed, held, sems
):
    outers = (packed_own, before, after, packed_mate, mate_before, mate_after)
    loads = loaded(own, mate, outers, (weight_two, weight_one), full, packed, held, sems)
    build(full, packed, 0, picker(pick_ref, 0), frame, 0)
    loads[0].wait()
    output[0] = convolved(frame, held.at[0]).astype(BF16)
    build(full, packed, 1, picker(pick_ref, 0), frame, 0)
    loads[1].wait()
    grad_input[0] = convolved_turned(frame, held.at[1]).astype(BF16)


def gradient_kernel(place_ref, both, both_mate, frames, passed, *rest):
    parts, (turned, blocks) = rest[0:5], rest[6:]
    core = place_ref[0]
    turned[0] = both[core].T
    turned[1] = both_mate[core].T

    def run(core):
        for plane in range(3):
            for third in range(3):
                lanes = slice(third * 3 * CH, (third + 1) * 3 * CH)
                row = 64 * plane
                total = jnp.dot(turned[0], frames[row : row + ROWS, lanes], preferred_element_type=F32)
                row += FRAME_ROWS
                total += jnp.dot(turned[1], frames[row : row + ROWS, lanes], preferred_element_type=F32)
                for tap in range(3):
                    k = 9 * plane + 3 * third + tap
                    block = total[:, tap * CH : (tap + 1) * CH].astype(BF16)
                    if core == 0:
                        blocks[26 - k] = block
                    else:
                        blocks[k] = block.T

    @pl.when(core == 0)
    def _():
        run(0)

    @pl.when(core != 0)
    def _():
        run(1)

    for step, part in zip((0, 1, 3), parts[0:3]):
        part[...] = blocks[:, whole_rows(place_ref[1] + step), :]
    for other, part in enumerate(parts[3:5]):
        part[...] = blocks[:, half_rows(place_ref[1] + 2, place_ref[4] + other), :]


def whole_rows(along):
    return pl.ds(pl.multiple_of((along % 4) * 64, 64), 64)


def half_rows(along, bit):
    return pl.ds(pl.multiple_of((along % 4) * 64 + (bit % 2) * 32, 32), 32)


def scatter_kernel(place_ref, own, after, before, across, *outs):
    for step in range(4):
        quarter = (place_ref[3] + step) % 4
        rows = pl.ds(pl.multiple_of(quarter * 16, 16), 16)
        half = pl.ds(pl.multiple_of((quarter % 2) * 16, 16), 16)
        total = own[:, rows, :].astype(F32) + after[:, rows, :].astype(F32) + before[:, rows, :].astype(F32)
        two_on = across[:, half, :].astype(F32)
        total += jnp.where(quarter // 2 == place_ref[4], two_on, jnp.zeros_like(two_on))
        outs[step][...] = total.astype(BF16)


def gather_kernel(place_ref, part0, part1, part2, part3, passed, wide, again, half, passed_out):
    for step, part in enumerate((part0, part1, part2, part3)):
        quarter = (place_ref[3] + 4 - step) % 4
        rows = pl.ds(pl.multiple_of(quarter * 16, 16), 16)
        wide[:, rows, :] = part[...]
        again[:, rows, :] = part[...]

        @pl.when(quarter // 2 == place_ref[4])
        def _(part=part, quarter=quarter):
            half[:, pl.ds(pl.multiple_of((quarter % 2) * 16, 16), 16), :] = part[...]


def place_kernel(hows, place_ref, *refs):
    count = len(hows)
    own, mate = refs[0:count], refs[count : 2 * count]
    grad_one, grad_two, sems = refs[-3:]

    def run(own_dst, mate_dst):
        made = []
        for n, (how, other) in enumerate(hows):
            for side, (dst, part) in enumerate(((own_dst, own[n]), (mate_dst, mate[n]))):
                along, bit = place_ref[1 + side], place_ref[4 + side]
                rows = whole_rows(along + how) if how != 2 else half_rows(along + 2, bit + other)
                made.append(pltpu.make_async_copy(part, dst.at[:, rows, :], sems.at[side, n]))
        for copy in made:
            copy.start()
        for copy in made:
            copy.wait()

    @pl.when(place_ref[0] == 0)
    def _():
        run(grad_two, grad_one)

    @pl.when(place_ref[0] != 0)
    def _():
        run(grad_one, grad_two)


def call(kernel, name, outs, in_specs, out_specs, scratch, flops, moved, mib, aliases=None):
    return pl.pallas_call(
        kernel,
        name=name,
        out_shape=[
            jax.ShapeDtypeStruct(*out) if isinstance(out[0], tuple) else jax.ShapeDtypeStruct(out, BF16)
            for out in outs
        ],
        in_specs=in_specs,
        out_specs=out_specs,
        scratch_shapes=scratch,
        input_output_aliases=aliases or {},
        compiler_params=pltpu.CompilerParams(vmem_limit_bytes=mib * 1024 * 1024),
        cost_estimate=pl.CostEstimate(flops=flops, bytes_accessed=moved, transcendentals=0),
    )


def on_device(
    features, cotangent, weight_one, weight_two, occupancy, neighbour_owner, neighbour_slot
):
    index = lax.axis_index(AXES)
    here = coordinates(index)
    core = here["core"]
    first, second, third = ("x", "z"), ("z", "y"), ("y", "x")

    def along(axis, which):
        return jnp.where(which == 0, here[axis[0]], here[axis[1]])

    bits = jnp.stack([here["y"] % 2, here["y"] // 2])
    pairing = (EVEN, ODD)
    place = jnp.stack(
        [core, along(first, core), along(first, 1 - core), along(second, core), bits[core], bits[1 - core]]
    )
    place = place.astype(jnp.int32)

    graph = jnp.concatenate([occupancy.reshape(1, 1), neighbour_owner], axis=1)
    graph_mate = swap(graph)
    two = jnp.concatenate([graph, graph_mate], axis=0)
    first_brick = index - core - 2
    own_brick = jnp.stack([index, index ^ 1])[:, None]
    own_brick = jnp.where(two[:, 0:1] > 0, own_brick, -1)
    owners = jnp.concatenate([two[:, 1:14], own_brick, two[:, 14:27]], axis=1)
    rel = owners - first_brick
    same = (rel % 2) == core
    kind = jnp.where(rel // 2 == 1, 0, jnp.where(rel // 2 == 0, 1, 2))
    picks = jnp.where(owners >= 0, jnp.where(same, kind, kind + 3), 6).astype(jnp.int32)

    def sent_halo(field):
        return shifted(field, 2), shifted(field, -2)

    flops = 2 * ROWS * TAPS * 3 * CH
    full = pltpu.VMEM((2, 3, ROWS, CH), BF16)
    packed = pltpu.VMEM((2, 7, OUTER, CH), BF16)
    frame = pltpu.VMEM((FRAME_ROWS, TAPS), BF16)
    held = pltpu.VMEM((2, 27, CH, CH), BF16)
    sems = pltpu.SemaphoreType.DMA((10,))
    pair, skin = (2, ROWS, CH), (2, OUTER, CH)
    rows64, rows32, rows16 = (27, 64, CH), (27, 32, CH), (27, 16, CH)

    fields, skins = call(
        pack_kernel, "pack_fields", [pair, skin], [VMEM_SPEC] * 2, [VMEM_SPEC] * 2, [], 1000, 1_000_000, 60,
    )(features, cotangent)
    before, after = sent_halo(skins)
    frames, spare = call(
        frames_kernel, "build_frames", [(2 * FRAME_ROWS, TAPS), (FRAME_ROWS, TAPS)],
        [SMEM_SPEC] * 2 + [ANY_SPEC] * 8, [VMEM_SPEC] * 2, [full, packed, sems], 1_000_000, 12_000_000, 14,
    )(picks, place, fields, swap(fields), skins, before, after, swap(skins), swap(before), swap(after))
    (pre_act,) = call(
        hidden_kernel, "first_conv", [((ROWS, CH), F32)], [SMEM_SPEC] + [VMEM_SPEC] * 3, [VMEM_SPEC], [],
        flops, 4_000_000, 14,
    )(place, frames, spare, weight_one)
    (both,) = call(
        grad_kernel, "grad_conv", [pair], [SMEM_SPEC] + [VMEM_SPEC] * 4, [VMEM_SPEC], [],
        flops, 4_000_000, 14,
    )(place, frames, spare, weight_two, pre_act)
    both_mate = swap(both)

    *parts, both = call(
        gradient_kernel, "weight_grads", [rows64] * 3 + [rows32] * 2 + [pair],
        [SMEM_SPEC] + [VMEM_SPEC] * 3 + [ANY_SPEC], [VMEM_SPEC] * 5 + [ANY_SPEC],
        [pltpu.VMEM((2, CH, ROWS), BF16), pltpu.VMEM((27, CH, CH), BF16)],
        2 * flops, 10_000_000, 18, {4: 5},
    )(place, both, both_mate, frames, both)

    def rounds(arrays, axis):
        return [arrays[0]] + [ring_send(arrays[d], axis, d) for d in (1, 2, 3)]

    own, to_after, to_before, kept, given = parts
    across = kept.astype(F32) + ring_send(given, first, 0, pairing).astype(F32)
    arrived = [
        own,
        ring_send(to_after, first, 1),
        ring_send(to_before, first, 3),
        ring_send(across.astype(BF16), first, 2),
    ]
    quarter = call(
        scatter_kernel, "sum_and_split", [rows16] * 4, [SMEM_SPEC] + [VMEM_SPEC] * 4, [VMEM_SPEC] * 4,
        [], 4_000_000, 4_500_000, 12,
    )(place, *arrived)

    (skins,) = call(
        pack_both_kernel, "pack_both", [skin], [VMEM_SPEC, ANY_SPEC], [VMEM_SPEC], [], 1000, 1_000_000, 8,
    )(both, quarter[0])
    before, after = sent_halo(skins)
    mate_before, mate_after = swap(before), swap(after)
    skins_mate = swap(skins)
    def added(arrays):
        wide = [array.astype(F32) for array in arrays]
        return (wide[0] + wide[2]) + (wide[1] + wide[3])

    small = added(rounds(quarter, second)).astype(BF16)
    scale = float(128 * ROWS) ** (-0.5)
    whole = (scale * added(rounds([small] * 4, third))).astype(BF16)

    wide, again, half, both = call(
        gather_kernel, "gather_rows", [rows64] * 2 + [rows32, pair],
        [SMEM_SPEC] + [VMEM_SPEC] * 4 + [ANY_SPEC], [VMEM_SPEC] * 3 + [ANY_SPEC], [],
        1000, 2_700_000, 12, {5: 3},
    )(place, *rounds([whole] * 4, second), both)
    half = ring_send(half, first, 2)
    other_half = ring_send(half, first, 0, pairing)
    from_before, from_after = ring_send(wide, first, 1), ring_send(wide, first, 3)
    output, grad_input, again = call(
        outer_kernel, "outer_convs", [(1, ROWS, CH)] * 2 + [rows64],
        [SMEM_SPEC] + [ANY_SPEC] * 8 + [HBM_SPEC] * 2 + [ANY_SPEC], [VMEM_SPEC] * 2 + [ANY_SPEC],
        [frame, full, packed, held, sems], 2 * flops, 12_000_000, 18, {11: 2},
    )(picks, both, both_mate, skins, before, after, skins_mate, mate_before, mate_after, weight_two, weight_one, again)
    early = [(0, 0), (2, 0)]
    late = [(3, 0), (1, 0), (2, 1)]
    grad_one, grad_two = call(
        partial(place_kernel, early), "place_early", [(27, CH, CH)] * 2,
        [SMEM_SPEC] + [VMEM_SPEC] * 4, [ANY_SPEC] * 2,
        [pltpu.SemaphoreType.DMA((2, 2))], 1000, 5_000_000, 12,
    )(place, wide, half, swap(again), swap(half))
    chunks = [from_before, from_after, other_half]
    grad_one, grad_two = call(
        partial(place_kernel, late), "place_late", [(27, CH, CH)] * 2,
        [SMEM_SPEC] + [VMEM_SPEC] * 6 + [ANY_SPEC] * 2, [ANY_SPEC] * 2,
        [pltpu.SemaphoreType.DMA((2, 3))], 1000, 9_000_000, 12, {7: 0, 8: 1},
    )(place, *chunks, *[swap(chunk) for chunk in chunks], grad_one, grad_two)
    return output, grad_input, grad_one, grad_two


def solution(mesh):
    by_brick = P(AXES, None, None)
    in_specs = (by_brick, by_brick, P(), P(), P(AXES), P(AXES, None), P(AXES, None))
    out_specs = (by_brick, by_brick, P(), P())
    return jax.shard_map(
        on_device, mesh=mesh, in_specs=in_specs, out_specs=out_specs, check_vma=False
    )
```

```python
from functools import partial

import jax
import jax.numpy as jnp
from jax import lax
from jax.experimental import pallas as pl
from jax.experimental.pallas import tpu as pltpu
from jax.sharding import PartitionSpec as P

AXES = ("region", "shard")
SIDES = (4, 4, 4, 2)
ROWS = 512
OUTER = 320
CH = 256
TAPS = 2304
FRAME_ROWS = 640
EVEN = (1, 0, 3, 2)
ODD = (3, 2, 1, 0)
F32 = jnp.float32
BF16 = jnp.bfloat16
VMEM_SPEC = pl.BlockSpec(memory_space=pltpu.VMEM)
SMEM_SPEC = pl.BlockSpec(memory_space=pltpu.SMEM)
ANY_SPEC = pl.BlockSpec(memory_space=pl.ANY)
HBM_SPEC = pl.BlockSpec(memory_space=pltpu.HBM)


def coordinates(index):
    return {"x": index // 32, "z": (index // 8) % 4, "y": (index // 2) % 4, "core": index % 2}


def device_at(place):
    return place["x"] * 32 + place["z"] * 8 + place["y"] * 2 + place["core"]


def ring_send(array, axis_of_core, step, pairing=(None, None)):
    pairs = []
    for index in range(128):
        place = coordinates(index)
        axis = axis_of_core[place["core"]]
        place[axis] = (place[axis] + step) % 4
        partner = pairing[place["core"]]
        place["y"] = partner[place["y"]] if partner else place["y"]
        pairs.append((index, device_at(place)))
    return lax.ppermute(array, AXES, pairs)


def swap(array):
    return lax.ppermute(array, AXES, [(index, index ^ 1) for index in range(128)])


def shifted(array, by):
    return lax.ppermute(array, AXES, [(i, i + by) for i in range(128) if 0 <= i + by < 128])


def pack(brick, packed, field):
    packed[field, 0:64] = brick[0:64]
    packed[field, 64:128] = brick[448:512]
    for x in range(1, 7):
        slab = brick[64 * x : 64 * x + 64].astype(F32).reshape(8, 8, CH)
        edges = jnp.concatenate([slab[0], slab[7], slab[:, 0, :], slab[:, 7, :]], axis=0)
        packed[field, 96 + 32 * x : 128 + 32 * x] = edges.astype(BF16)


def build(full, packed, field, pick, out, first_row):
    z_of = lax.broadcasted_iota(jnp.int32, (10, 8, CH), 1)
    centre = pick(1, 1, 1) // 3

    def outer(sx, sy, sz, first, count):
        return packed[field, pick(sx, sy, sz), pl.ds(first, count), :].astype(F32)

    def plane(X, columns):
        below, here, above = [
            jnp.concatenate([low[None], mid, high[None]], axis=0) for low, mid, high in columns
        ]
        shifts = (
            pltpu.roll(jnp.where(z_of == 7, below, here), 1, 1),
            here,
            pltpu.roll(jnp.where(z_of == 0, above, here), 7, 1),
        )
        rows = pl.ds(pl.multiple_of(first_row + X * 64, 64), 64)
        for dz, grid in enumerate(shifts):
            even = grid.reshape(80, CH).astype(BF16)
            odd = grid[1:9].reshape(64, CH).astype(BF16)
            out[rows, (0 + dz) * CH : (1 + dz) * CH] = even[0:64]
            out[rows, (3 + dz) * CH : (4 + dz) * CH] = odd
            out[rows, (6 + dz) * CH : (7 + dz) * CH] = even[16:80]

    def inside(xp):
        return full[field, centre, pl.ds(pl.multiple_of(xp * 64, 64), 64), :].astype(F32).reshape(8, 8, CH)

    for X, sx, face in ((0, 0, 64), (1, 1, 0), (8, 1, 64), (9, 2, 0)):
        columns = []
        for sz in range(3):
            if sx == 1 and sz == 1:
                mid = inside(X - 1)
            else:
                mid = outer(sx, 1, sz, face, 64).reshape(8, 8, CH)
            columns.append((outer(sx, 0, sz, face + 48, 16)[8:16], mid, outer(sx, 2, sz, face, 16)[0:8]))
        plane(X, columns)

    @pl.loop(2, 8)
    def _(X):
        first = pl.multiple_of(64 + 32 * X, 32)
        columns = []
        for sz in range(3):
            if sz == 1:
                mid = inside(X - 1)
            else:
                edge = outer(1, 1, sz, first + 16, 16)
                edge = edge[8:16] if sz == 0 else edge[0:8]
                mid = jnp.broadcast_to(edge[:, None, :], (8, 8, CH))
            columns.append((outer(1, 0, sz, first, 16)[8:16], mid, outer(1, 2, sz, first, 16)[0:8]))
        plane(X, columns)


def convolved(frame, weights):
    total = None
    for plane in range(3):
        term = jnp.dot(
            frame[64 * plane : 64 * plane + ROWS, :],
            weights[9 * plane : 9 * plane + 9].reshape(TAPS, CH),
            preferred_element_type=F32,
        )
        total = term if total is None else total + term
    return total


def convolved_turned(frame, weights):
    total = None
    for k in range(27):
        window = frame[64 * (k // 9) : 64 * (k // 9) + ROWS, (k % 9) * CH : (k % 9 + 1) * CH]
        term = lax.dot_general(
            window, weights[26 - k], (((1,), (1,)), ((), ())), preferred_element_type=F32
        )
        total = term if total is None else total + term
    return total


def picker(pick_ref, which):
    return lambda sx, sy, sz: pick_ref[which, 9 * sx + 3 * sy + sz]


def loaded(own, mate, outers, weights, full, packed, held, sems):
    copies = [
        pltpu.make_async_copy(brick, full.at[:, place], sems.at[place])
        for place, brick in enumerate((own, mate))
    ]
    copies += [
        pltpu.make_async_copy(brick, packed.at[:, place], sems.at[2 + place])
        for place, brick in enumerate(outers)
    ]
    loads = [
        pltpu.make_async_copy(weight, held.at[place], sems.at[8 + place])
        for place, weight in enumerate(weights)
    ]
    for copy in copies + loads:
        copy.start()
    full[:, 2] = jnp.zeros((2, ROWS, CH), BF16)
    packed[:, 6] = jnp.zeros((2, OUTER, CH), BF16)
    for copy in copies:
        copy.wait()
    return loads


def order_kernel(passed, waited_for, passed_out):
    pass


def pack_kernel(features, cotangent, out, packed):
    for place, field in enumerate((features, cotangent)):
        out[place] = field[0]
        pack(field.at[0], packed, place)


def pack_both_kernel(both, waited_for, packed):
    for place in range(2):
        pack(both.at[place], packed, place)


def pack_mate_kernel(mate, packed):
    for place in range(2):
        pack(mate.at[place], packed, place)


def frames_kernel(
    pick_ref, place_ref, own, mate, packed_own, before, after, packed_mate, mate_before, mate_after,
    frames, spare, full, packed, sems
):
    outers = (packed_own, before, after, packed_mate, mate_before, mate_after)
    loaded(own, mate, outers, (), full, packed, None, sems)
    core = place_ref[0]
    build(full, packed, 1 - core, picker(pick_ref, 0), frames, 0)
    build(full, packed, core, picker(pick_ref, 0), spare, 0)
    build(full, packed, 1 - core, picker(pick_ref, 1), frames, FRAME_ROWS)


def hidden_kernel(place_ref, frames, spare, weight_one, pre_act):
    @pl.when(place_ref[0] == 0)
    def _():
        pre_act[...] = convolved(spare, weight_one)

    @pl.when(place_ref[0] != 0)
    def _():
        pre_act[...] = convolved(frames, weight_one)


def grad_kernel(place_ref, frames, spare, weight_two, pre_act_ref, both):
    def finish(frame):
        grad_hidden = convolved_turned(frame, weight_two)
        pre_act = pre_act_ref[...]
        sig = 1.0 / (1.0 + jnp.exp(-pre_act))
        both[0] = (pre_act / (1.0 + jnp.exp(-pre_act))).astype(BF16)
        both[1] = (grad_hidden * sig * (1.0 + pre_act * (1.0 - sig))).astype(BF16)

    @pl.when(place_ref[0] == 0)
    def _():
        finish(frames)

    @pl.when(place_ref[0] != 0)
    def _():
        finish(spare)


def outer_frames_kernel(
    pick_ref, own, mate, packed_own, before, after, packed_mate, mate_before, mate_after, waited_for,
    frame_hidden, frame_grad, full, packed, sems
):
    outers = (packed_own, before, after, packed_mate, mate_before, mate_after)
    loaded(own, mate, outers, (), full, packed, None, sems)
    build(full, packed, 0, picker(pick_ref, 0), frame_hidden, 0)
    build(full, packed, 1, picker(pick_ref, 0), frame_grad, 0)


def output_kernel(frame, weight_two, passed, output, passed_out):
    output[0] = convolved(frame, weight_two).astype(BF16)


def grad_input_kernel(frame, weight_one, passed, grad_input, passed_out):
    grad_input[0] = convolved_turned(frame, weight_one).astype(BF16)


def gradient_kernel(place_ref, both, both_mate, frames, passed, *rest):
    parts, (turned, blocks) = rest[0:5], rest[6:]
    core = place_ref[0]
    turned[0] = both[core].T
    turned[1] = both_mate[core].T

    def run(core):
        for plane in range(3):
            for third in range(3):
                lanes = slice(third * 3 * CH, (third + 1) * 3 * CH)
                row = 64 * plane
                total = jnp.dot(turned[0], frames[row : row + ROWS, lanes], preferred_element_type=F32)
                row += FRAME_ROWS
                total += jnp.dot(turned[1], frames[row : row + ROWS, lanes], preferred_element_type=F32)
                for tap in range(3):
                    k = 9 * plane + 3 * third + tap
                    block = total[:, tap * CH : (tap + 1) * CH].astype(BF16)
                    if core == 0:
                        blocks[26 - k] = block
                    else:
                        blocks[k] = block.T

    @pl.when(core == 0)
    def _():
        run(0)

    @pl.when(core != 0)
    def _():
        run(1)

    for step, part in zip((0, 1, 3), parts[0:3]):
        part[...] = blocks[:, whole_rows(place_ref[1] + step), :]
    for other, part in enumerate(parts[3:5]):
        part[...] = blocks[:, half_rows(place_ref[1] + 2, place_ref[4] + other), :]


def whole_rows(along):
    return pl.ds(pl.multiple_of((along % 4) * 64, 64), 64)


def half_rows(along, bit):
    return pl.ds(pl.multiple_of((along % 4) * 64 + (bit % 2) * 32, 32), 32)


def scatter_kernel(place_ref, own, after, before, across, *outs):
    for step in range(4):
        quarter = (place_ref[3] + step) % 4
        rows = pl.ds(pl.multiple_of(quarter * 16, 16), 16)
        half = pl.ds(pl.multiple_of((quarter % 2) * 16, 16), 16)
        total = own[:, rows, :].astype(F32) + after[:, rows, :].astype(F32) + before[:, rows, :].astype(F32)
        two_on = across[:, half, :].astype(F32)
        total += jnp.where(quarter // 2 == place_ref[4], two_on, jnp.zeros_like(two_on))
        outs[step][...] = total.astype(BF16)


def gather_kernel(place_ref, part0, part1, part2, part3, passed, wide, again, half, passed_out):
    for step, part in enumerate((part0, part1, part2, part3)):
        quarter = (place_ref[3] + 4 - step) % 4
        rows = pl.ds(pl.multiple_of(quarter * 16, 16), 16)
        wide[:, rows, :] = part[...]
        again[:, rows, :] = part[...]

        @pl.when(quarter // 2 == place_ref[4])
        def _(part=part, quarter=quarter):
            half[:, pl.ds(pl.multiple_of((quarter % 2) * 16, 16), 16), :] = part[...]


def place_kernel(hows, place_ref, *refs):
    count = len(hows)
    own, mate = refs[0:count], refs[count : 2 * count]
    grad_one, grad_two, sems = refs[-3:]

    def run(own_dst, mate_dst):
        made = []
        for n, (how, other) in enumerate(hows):
            for side, (dst, part) in enumerate(((own_dst, own[n]), (mate_dst, mate[n]))):
                along, bit = place_ref[1 + side], place_ref[4 + side]
                rows = whole_rows(along + how) if how != 2 else half_rows(along + 2, bit + other)
                made.append(pltpu.make_async_copy(part, dst.at[:, rows, :], sems.at[side, n]))
        for copy in made:
            copy.start()
        for copy in made:
            copy.wait()

    @pl.when(place_ref[0] == 0)
    def _():
        run(grad_two, grad_one)

    @pl.when(place_ref[0] != 0)
    def _():
        run(grad_one, grad_two)


def call(kernel, name, outs, in_specs, out_specs, scratch, flops, moved, mib, aliases=None):
    return pl.pallas_call(
        kernel,
        name=name,
        out_shape=[
            jax.ShapeDtypeStruct(*out) if isinstance(out[0], tuple) else jax.ShapeDtypeStruct(out, BF16)
            for out in outs
        ],
        in_specs=in_specs,
        out_specs=out_specs,
        scratch_shapes=scratch,
        input_output_aliases=aliases or {},
        compiler_params=pltpu.CompilerParams(vmem_limit_bytes=mib * 1024 * 1024),
        cost_estimate=pl.CostEstimate(flops=flops, bytes_accessed=moved, transcendentals=0),
    )


def on_device(
    features, cotangent, weight_one, weight_two, occupancy, neighbour_owner, neighbour_slot
):
    index = lax.axis_index(AXES)
    here = coordinates(index)
    core = here["core"]
    first, second, third = ("x", "z"), ("z", "y"), ("y", "x")

    def along(axis, which):
        return jnp.where(which == 0, here[axis[0]], here[axis[1]])

    bits = jnp.stack([here["y"] % 2, here["y"] // 2])
    pairing = (EVEN, ODD)
    place = jnp.stack(
        [core, along(first, core), along(first, 1 - core), along(second, core), bits[core], bits[1 - core]]
    )
    place = place.astype(jnp.int32)

    graph = jnp.concatenate([occupancy.reshape(1, 1), neighbour_owner], axis=1)
    graph_mate = swap(graph)
    two = jnp.concatenate([graph, graph_mate], axis=0)
    first_brick = index - core - 2
    own_brick = jnp.stack([index, index ^ 1])[:, None]
    own_brick = jnp.where(two[:, 0:1] > 0, own_brick, -1)
    owners = jnp.concatenate([two[:, 1:14], own_brick, two[:, 14:27]], axis=1)
    rel = owners - first_brick
    same = (rel % 2) == core
    kind = jnp.where(rel // 2 == 1, 0, jnp.where(rel // 2 == 0, 1, 2))
    picks = jnp.where(owners >= 0, jnp.where(same, kind, kind + 3), 6).astype(jnp.int32)

    def sent_halo(field):
        return shifted(field, 2), shifted(field, -2)

    flops = 2 * ROWS * TAPS * 3 * CH
    full = pltpu.VMEM((2, 3, ROWS, CH), BF16)
    packed = pltpu.VMEM((2, 7, OUTER, CH), BF16)
    frame = pltpu.VMEM((FRAME_ROWS, TAPS), BF16)
    held = pltpu.VMEM((2, 27, CH, CH), BF16)
    sems = pltpu.SemaphoreType.DMA((10,))
    pair, skin = (2, ROWS, CH), (2, OUTER, CH)
    rows64, rows32, rows16 = (27, 64, CH), (27, 32, CH), (27, 16, CH)

    fields, skins = call(
        pack_kernel, "pack_fields", [pair, skin], [VMEM_SPEC] * 2, [VMEM_SPEC] * 2, [], 1000, 1_000_000, 60,
    )(features, cotangent)
    before, after = sent_halo(skins)

    def packed_mate(mate):
        return call(
            pack_mate_kernel, "pack_mate", [skin], [VMEM_SPEC], [VMEM_SPEC], [], 1000, 1_000_000, 8
        )(mate)[0]

    mate = swap(fields)
    frames, spare = call(
        frames_kernel, "build_frames", [(2 * FRAME_ROWS, TAPS), (FRAME_ROWS, TAPS)],
        [SMEM_SPEC] * 2 + [ANY_SPEC] * 8, [VMEM_SPEC] * 2, [full, packed, sems], 1_000_000, 12_000_000, 14,
    )(picks, place, fields, mate, skins, before, after, packed_mate(mate), swap(before), swap(after))
    (pre_act,) = call(
        hidden_kernel, "first_conv", [((ROWS, CH), F32)], [SMEM_SPEC] + [VMEM_SPEC] * 3, [VMEM_SPEC], [],
        flops, 4_000_000, 14,
    )(place, frames, spare, weight_one)
    (both,) = call(
        grad_kernel, "grad_conv", [pair], [SMEM_SPEC] + [VMEM_SPEC] * 4, [VMEM_SPEC], [],
        flops, 4_000_000, 14,
    )(place, frames, spare, weight_two, pre_act)
    both_mate = swap(both)

    *parts, both = call(
        gradient_kernel, "weight_grads", [rows64] * 3 + [rows32] * 2 + [pair],
        [SMEM_SPEC] + [VMEM_SPEC] * 3 + [ANY_SPEC], [VMEM_SPEC] * 5 + [ANY_SPEC],
        [pltpu.VMEM((2, CH, ROWS), BF16), pltpu.VMEM((27, CH, CH), BF16)],
        2 * flops, 10_000_000, 18, {4: 5},
    )(place, both, both_mate, frames, both)

    def rounds(arrays, axis):
        return [arrays[0]] + [ring_send(arrays[d], axis, d) for d in (1, 2, 3)]

    own, to_after, to_before, kept, given = parts
    across = kept.astype(F32) + ring_send(given, first, 0, pairing).astype(F32)
    arrived = [
        own,
        ring_send(to_after, first, 1),
        ring_send(to_before, first, 3),
        ring_send(across.astype(BF16), first, 2),
    ]
    quarter = call(
        scatter_kernel, "sum_and_split", [rows16] * 4, [SMEM_SPEC] + [VMEM_SPEC] * 4, [VMEM_SPEC] * 4,
        [], 4_000_000, 4_500_000, 12,
    )(place, *arrived)

    (skins,) = call(
        pack_both_kernel, "pack_both", [skin], [VMEM_SPEC, ANY_SPEC], [VMEM_SPEC], [], 1000, 1_000_000, 8,
    )(both, quarter[0])
    before, after = sent_halo(skins)
    mate_before, mate_after = swap(before), swap(after)
    skins_mate = packed_mate(both_mate)
    def added(arrays):
        wide = [array.astype(F32) for array in arrays]
        return (wide[0] + wide[2]) + (wide[1] + wide[3])

    small = added(rounds(quarter, second)).astype(BF16)
    scale = float(128 * ROWS) ** (-0.5)
    whole = (scale * added(rounds([small] * 4, third))).astype(BF16)

    wide, again, half, both = call(
        gather_kernel, "gather_rows", [rows64] * 2 + [rows32, pair],
        [SMEM_SPEC] + [VMEM_SPEC] * 4 + [ANY_SPEC], [VMEM_SPEC] * 3 + [ANY_SPEC], [],
        1000, 2_700_000, 12, {5: 3},
    )(place, *rounds([whole] * 4, second), both)
    half = ring_send(half, first, 2)
    other_half = ring_send(half, first, 0, pairing)
    from_before, from_after = ring_send(wide, first, 1), ring_send(wide, first, 3)
    frame_hidden, frame_grad = call(
        outer_frames_kernel, "outer_frames", [(FRAME_ROWS, TAPS)] * 2, [SMEM_SPEC] + [ANY_SPEC] * 9,
        [VMEM_SPEC] * 2, [full, packed, sems], 1_000_000, 8_000_000, 14,
    )(picks, both, both_mate, skins, before, after, skins_mate, mate_before, mate_after, both)
    output, again = call(
        output_kernel, "output_conv", [(1, ROWS, CH), rows64], [VMEM_SPEC] * 2 + [ANY_SPEC],
        [VMEM_SPEC, ANY_SPEC], [], flops, 4_000_000, 14, {2: 1},
    )(frame_hidden, weight_two, again)
    grad_input, again = call(
        grad_input_kernel, "grad_input_conv", [(1, ROWS, CH), rows64], [VMEM_SPEC] * 2 + [ANY_SPEC],
        [VMEM_SPEC, ANY_SPEC], [], flops, 4_000_000, 14, {2: 1},
    )(frame_grad, weight_one, again)
    early = [(0, 0), (2, 0)]
    late = [(3, 0), (1, 0), (2, 1)]
    grad_one, grad_two = call(
        partial(place_kernel, early), "place_early", [(27, CH, CH)] * 2,
        [SMEM_SPEC] + [VMEM_SPEC] * 4, [ANY_SPEC] * 2,
        [pltpu.SemaphoreType.DMA((2, 2))], 1000, 5_000_000, 12,
    )(place, wide, half, swap(again), swap(half))
    chunks = [from_before, from_after, other_half]
    grad_one, grad_two = call(
        partial(place_kernel, late), "place_late", [(27, CH, CH)] * 2,
        [SMEM_SPEC] + [VMEM_SPEC] * 6 + [ANY_SPEC] * 2, [ANY_SPEC] * 2,
        [pltpu.SemaphoreType.DMA((2, 3))], 1000, 9_000_000, 12, {7: 0, 8: 1},
    )(place, *chunks, *[swap(chunk) for chunk in chunks], grad_one, grad_two)
    return output, grad_input, grad_one, grad_two


def solution(mesh):
    by_brick = P(AXES, None, None)
    in_specs = (by_brick, by_brick, P(), P(), P(AXES), P(AXES, None), P(AXES, None))
    out_specs = (by_brick, by_brick, P(), P())
    return jax.shard_map(
        on_device, mesh=mesh, in_specs=in_specs, out_specs=out_specs, check_vma=False
    )
```

```python
from functools import partial

import jax
import jax.numpy as jnp
from jax import lax
from jax.experimental import pallas as pl
from jax.experimental.pallas import tpu as pltpu
from jax.sharding import PartitionSpec as P

AXES = ("region", "shard")
SIDES = (4, 4, 4, 2)
ROWS = 512
OUTER = 320
CH = 256
TAPS = 2304
FRAME_ROWS = 640
EVEN = (1, 0, 3, 2)
ODD = (3, 2, 1, 0)
F32 = jnp.float32
BF16 = jnp.bfloat16
VMEM_SPEC = pl.BlockSpec(memory_space=pltpu.VMEM)
SMEM_SPEC = pl.BlockSpec(memory_space=pltpu.SMEM)
ANY_SPEC = pl.BlockSpec(memory_space=pl.ANY)
HBM_SPEC = pl.BlockSpec(memory_space=pltpu.HBM)


def coordinates(index):
    return {"x": index // 32, "z": (index // 8) % 4, "y": (index // 2) % 4, "core": index % 2}


def device_at(place):
    return place["x"] * 32 + place["z"] * 8 + place["y"] * 2 + place["core"]


def ring_send(array, axis_of_core, step, pairing=(None, None)):
    pairs = []
    for index in range(128):
        place = coordinates(index)
        axis = axis_of_core[place["core"]]
        place[axis] = (place[axis] + step) % 4
        partner = pairing[place["core"]]
        place["y"] = partner[place["y"]] if partner else place["y"]
        pairs.append((index, device_at(place)))
    return lax.ppermute(array, AXES, pairs)


def swap(array):
    return lax.ppermute(array, AXES, [(index, index ^ 1) for index in range(128)])


def shifted(array, by):
    return lax.ppermute(array, AXES, [(i, i + by) for i in range(128) if 0 <= i + by < 128])


def pack(brick, packed, field):
    packed[field, 0:64] = brick[0:64]
    packed[field, 64:128] = brick[448:512]
    for x in range(1, 7):
        slab = brick[64 * x : 64 * x + 64].astype(F32).reshape(8, 8, CH)
        edges = jnp.concatenate([slab[0], slab[7], slab[:, 0, :], slab[:, 7, :]], axis=0)
        packed[field, 96 + 32 * x : 128 + 32 * x] = edges.astype(BF16)


def build(full, packed, field, pick, out, first_row):
    z_of = lax.broadcasted_iota(jnp.int32, (10, 8, CH), 1)
    centre = pick(1, 1, 1) // 3

    def outer(sx, sy, sz, first, count):
        return packed[field, pick(sx, sy, sz), pl.ds(first, count), :].astype(F32)

    def plane(X, columns):
        below, here, above = [
            jnp.concatenate([low[None], mid, high[None]], axis=0) for low, mid, high in columns
        ]
        shifts = (
            pltpu.roll(jnp.where(z_of == 7, below, here), 1, 1),
            here,
            pltpu.roll(jnp.where(z_of == 0, above, here), 7, 1),
        )
        rows = pl.ds(pl.multiple_of(first_row + X * 64, 64), 64)
        for dz, grid in enumerate(shifts):
            even = grid.reshape(80, CH).astype(BF16)
            odd = grid[1:9].reshape(64, CH).astype(BF16)
            out[rows, (0 + dz) * CH : (1 + dz) * CH] = even[0:64]
            out[rows, (3 + dz) * CH : (4 + dz) * CH] = odd
            out[rows, (6 + dz) * CH : (7 + dz) * CH] = even[16:80]

    def inside(xp):
        return full[field, centre, pl.ds(pl.multiple_of(xp * 64, 64), 64), :].astype(F32).reshape(8, 8, CH)

    for X, sx, face in ((0, 0, 64), (1, 1, 0), (8, 1, 64), (9, 2, 0)):
        columns = []
        for sz in range(3):
            if sx == 1 and sz == 1:
                mid = inside(X - 1)
            else:
                mid = outer(sx, 1, sz, face, 64).reshape(8, 8, CH)
            columns.append((outer(sx, 0, sz, face + 48, 16)[8:16], mid, outer(sx, 2, sz, face, 16)[0:8]))
        plane(X, columns)

    @pl.loop(2, 8)
    def _(X):
        first = pl.multiple_of(64 + 32 * X, 32)
        columns = []
        for sz in range(3):
            if sz == 1:
                mid = inside(X - 1)
            else:
                edge = outer(1, 1, sz, first + 16, 16)
                edge = edge[8:16] if sz == 0 else edge[0:8]
                mid = jnp.broadcast_to(edge[:, None, :], (8, 8, CH))
            columns.append((outer(1, 0, sz, first, 16)[8:16], mid, outer(1, 2, sz, first, 16)[0:8]))
        plane(X, columns)


def convolved(frame, weights):
    total = None
    for plane in range(3):
        term = jnp.dot(
            frame[64 * plane : 64 * plane + ROWS, :],
            weights[9 * plane : 9 * plane + 9].reshape(TAPS, CH),
            preferred_element_type=F32,
        )
        total = term if total is None else total + term
    return total


def convolved_turned(frame, weights):
    total = None
    for k in range(27):
        window = frame[64 * (k // 9) : 64 * (k // 9) + ROWS, (k % 9) * CH : (k % 9 + 1) * CH]
        term = lax.dot_general(
            window, weights[26 - k], (((1,), (1,)), ((), ())), preferred_element_type=F32
        )
        total = term if total is None else total + term
    return total


def picker(pick_ref, which):
    return lambda sx, sy, sz: pick_ref[which, 9 * sx + 3 * sy + sz]


def loaded(own, mate, outers, weights, full, packed, held, sems):
    copies = [
        pltpu.make_async_copy(brick, full.at[:, place], sems.at[place])
        for place, brick in enumerate((own, mate))
    ]
    copies += [
        pltpu.make_async_copy(brick, packed.at[:, place], sems.at[2 + place])
        for place, brick in enumerate(outers)
    ]
    loads = [
        pltpu.make_async_copy(weight, held.at[place], sems.at[8 + place])
        for place, weight in enumerate(weights)
    ]
    for copy in copies + loads:
        copy.start()
    full[:, 2] = jnp.zeros((2, ROWS, CH), BF16)
    packed[:, 6] = jnp.zeros((2, OUTER, CH), BF16)
    for copy in copies:
        copy.wait()
    return loads


def order_kernel(passed, waited_for, passed_out):
    pass


def pack_kernel(features, cotangent, out, packed):
    for place, field in enumerate((features, cotangent)):
        out[place] = field[0]
        pack(field.at[0], packed, place)


def pack_both_kernel(both, waited_for, packed):
    for place in range(2):
        pack(both.at[place], packed, place)


def pack_mate_kernel(mate, packed):
    for place in range(2):
        pack(mate.at[place], packed, place)


def frames_kernel(
    pick_ref, place_ref, own, mate, packed_own, before, after, packed_mate, mate_before, mate_after,
    frames, spare, full, packed, sems
):
    outers = (packed_own, before, after, packed_mate, mate_before, mate_after)
    loaded(own, mate, outers, (), full, packed, None, sems)
    core = place_ref[0]
    build(full, packed, 1 - core, picker(pick_ref, 0), frames, 0)
    build(full, packed, core, picker(pick_ref, 0), spare, 0)
    build(full, packed, 1 - core, picker(pick_ref, 1), frames, FRAME_ROWS)


def hidden_kernel(place_ref, frames, spare, weight_one, pre_act):
    @pl.when(place_ref[0] == 0)
    def _():
        pre_act[...] = convolved(spare, weight_one)

    @pl.when(place_ref[0] != 0)
    def _():
        pre_act[...] = convolved(frames, weight_one)


def grad_kernel(place_ref, frames, spare, weight_two, pre_act_ref, both):
    def finish(frame):
        grad_hidden = convolved_turned(frame, weight_two)
        pre_act = pre_act_ref[...]
        sig = 1.0 / (1.0 + jnp.exp(-pre_act))
        both[0] = (pre_act / (1.0 + jnp.exp(-pre_act))).astype(BF16)
        both[1] = (grad_hidden * sig * (1.0 + pre_act * (1.0 - sig))).astype(BF16)

    @pl.when(place_ref[0] == 0)
    def _():
        finish(frames)

    @pl.when(place_ref[0] != 0)
    def _():
        finish(spare)


def outer_frames_kernel(
    pick_ref, own, mate, packed_own, before, after, packed_mate, mate_before, mate_after, waited_for,
    frame_hidden, frame_grad, full, packed, sems
):
    outers = (packed_own, before, after, packed_mate, mate_before, mate_after)
    loaded(own, mate, outers, (), full, packed, None, sems)
    build(full, packed, 0, picker(pick_ref, 0), frame_hidden, 0)
    build(full, packed, 1, picker(pick_ref, 0), frame_grad, 0)


def output_kernel(frame, weight_two, passed, output, passed_out):
    output[0] = convolved(frame, weight_two).astype(BF16)


def grad_input_kernel(frame, weight_one, passed, grad_input, passed_out):
    grad_input[0] = convolved_turned(frame, weight_one).astype(BF16)


def gradient_kernel(place_ref, both, both_mate, frames, passed, *rest):
    parts, (turned, blocks) = rest[0:5], rest[6:]
    core = place_ref[0]
    turned[0] = both[core].T
    turned[1] = both_mate[core].T

    def run(core):
        for plane in range(3):
            for third in range(3):
                lanes = slice(third * 3 * CH, (third + 1) * 3 * CH)
                row = 64 * plane
                total = jnp.dot(turned[0], frames[row : row + ROWS, lanes], preferred_element_type=F32)
                row += FRAME_ROWS
                total += jnp.dot(turned[1], frames[row : row + ROWS, lanes], preferred_element_type=F32)
                for tap in range(3):
                    k = 9 * plane + 3 * third + tap
                    block = total[:, tap * CH : (tap + 1) * CH].astype(BF16)
                    if core == 0:
                        blocks[26 - k] = block
                    else:
                        blocks[k] = block.T

    @pl.when(core == 0)
    def _():
        run(0)

    @pl.when(core != 0)
    def _():
        run(1)

    for step, part in zip((0, 1, 3), parts[0:3]):
        part[...] = blocks[:, whole_rows(place_ref[1] + step), :]
    for other, part in enumerate(parts[3:5]):
        part[...] = blocks[:, half_rows(place_ref[1] + 2, place_ref[4] + other), :]


def whole_rows(along):
    return pl.ds(pl.multiple_of((along % 4) * 64, 64), 64)


def half_rows(along, bit):
    return pl.ds(pl.multiple_of((along % 4) * 64 + (bit % 2) * 32, 32), 32)


def scatter_kernel(place_ref, own, after, before, across, *outs):
    for step in range(4):
        quarter = (place_ref[3] + step) % 4
        rows = pl.ds(pl.multiple_of(quarter * 16, 16), 16)
        half = pl.ds(pl.multiple_of((quarter % 2) * 16, 16), 16)
        total = own[:, rows, :].astype(F32) + after[:, rows, :].astype(F32) + before[:, rows, :].astype(F32)
        two_on = across[:, half, :].astype(F32)
        total += jnp.where(quarter // 2 == place_ref[4], two_on, jnp.zeros_like(two_on))
        outs[step][...] = total.astype(BF16)


def gather_kernel(place_ref, part0, part1, part2, part3, passed, wide, again, half, passed_out):
    for step, part in enumerate((part0, part1, part2, part3)):
        quarter = (place_ref[3] + 4 - step) % 4
        rows = pl.ds(pl.multiple_of(quarter * 16, 16), 16)
        wide[:, rows, :] = part[...]
        again[:, rows, :] = part[...]

        @pl.when(quarter // 2 == place_ref[4])
        def _(part=part, quarter=quarter):
            half[:, pl.ds(pl.multiple_of((quarter % 2) * 16, 16), 16), :] = part[...]


def place_kernel(hows, place_ref, *refs):
    count = len(hows)
    own, mate = refs[0:count], refs[count : 2 * count]
    grad_one, grad_two, sems = refs[-3:]

    def run(own_dst, mate_dst):
        made = []
        for n, (how, other) in enumerate(hows):
            for side, (dst, part) in enumerate(((own_dst, own[n]), (mate_dst, mate[n]))):
                along, bit = place_ref[1 + side], place_ref[4 + side]
                rows = whole_rows(along + how) if how != 2 else half_rows(along + 2, bit + other)
                made.append(pltpu.make_async_copy(part, dst.at[:, rows, :], sems.at[side, n]))
        for copy in made:
            copy.start()
        for copy in made:
            copy.wait()

    @pl.when(place_ref[0] == 0)
    def _():
        run(grad_two, grad_one)

    @pl.when(place_ref[0] != 0)
    def _():
        run(grad_one, grad_two)


def call(kernel, name, outs, in_specs, out_specs, scratch, flops, moved, mib, aliases=None):
    return pl.pallas_call(
        kernel,
        name=name,
        out_shape=[
            jax.ShapeDtypeStruct(*out) if isinstance(out[0], tuple) else jax.ShapeDtypeStruct(out, BF16)
            for out in outs
        ],
        in_specs=in_specs,
        out_specs=out_specs,
        scratch_shapes=scratch,
        input_output_aliases=aliases or {},
        compiler_params=pltpu.CompilerParams(vmem_limit_bytes=mib * 1024 * 1024),
        cost_estimate=pl.CostEstimate(flops=flops, bytes_accessed=moved, transcendentals=0),
    )


def on_device(
    features, cotangent, weight_one, weight_two, occupancy, neighbour_owner, neighbour_slot
):
    index = lax.axis_index(AXES)
    here = coordinates(index)
    core = here["core"]
    first, second, third = ("x", "z"), ("z", "y"), ("y", "x")

    def along(axis, which):
        return jnp.where(which == 0, here[axis[0]], here[axis[1]])

    bits = jnp.stack([here["y"] % 2, here["y"] // 2])
    pairing = (EVEN, ODD)
    place = jnp.stack(
        [core, along(first, core), along(first, 1 - core), along(second, core), bits[core], bits[1 - core]]
    )
    place = place.astype(jnp.int32)

    graph = jnp.concatenate([occupancy.reshape(1, 1), neighbour_owner], axis=1)
    graph_mate = swap(graph)
    two = jnp.concatenate([graph, graph_mate], axis=0)
    first_brick = index - core - 2
    own_brick = jnp.stack([index, index ^ 1])[:, None]
    own_brick = jnp.where(two[:, 0:1] > 0, own_brick, -1)
    owners = jnp.concatenate([two[:, 1:14], own_brick, two[:, 14:27]], axis=1)
    rel = owners - first_brick
    same = (rel % 2) == core
    kind = jnp.where(rel // 2 == 1, 0, jnp.where(rel // 2 == 0, 1, 2))
    picks = jnp.where(owners >= 0, jnp.where(same, kind, kind + 3), 6).astype(jnp.int32)

    def sent_halo(field):
        return shifted(field, 2), shifted(field, -2)

    flops = 2 * ROWS * TAPS * 3 * CH
    full = pltpu.VMEM((2, 3, ROWS, CH), BF16)
    packed = pltpu.VMEM((2, 7, OUTER, CH), BF16)
    frame = pltpu.VMEM((FRAME_ROWS, TAPS), BF16)
    held = pltpu.VMEM((2, 27, CH, CH), BF16)
    sems = pltpu.SemaphoreType.DMA((10,))
    pair, skin = (2, ROWS, CH), (2, OUTER, CH)
    rows64, rows32, rows16 = (27, 64, CH), (27, 32, CH), (27, 16, CH)

    fields, skins = call(
        pack_kernel, "pack_fields", [pair, skin], [VMEM_SPEC] * 2, [VMEM_SPEC] * 2, [], 1000, 1_000_000, 8,
    )(features, cotangent)
    before, after = sent_halo(skins)

    def packed_mate(mate):
        return call(
            pack_mate_kernel, "pack_mate", [skin], [VMEM_SPEC], [VMEM_SPEC], [], 1000, 1_000_000, 8
        )(mate)[0]

    mate = swap(fields)
    frames, spare = call(
        frames_kernel, "build_frames", [(2 * FRAME_ROWS, TAPS), (FRAME_ROWS, TAPS)],
        [SMEM_SPEC] * 2 + [ANY_SPEC] * 8, [VMEM_SPEC] * 2, [full, packed, sems], 1_000_000, 12_000_000, 14,
    )(picks, place, fields, mate, skins, before, after, packed_mate(mate), swap(before), swap(after))
    (pre_act,) = call(
        hidden_kernel, "first_conv", [((ROWS, CH), F32)], [SMEM_SPEC] + [VMEM_SPEC] * 3, [VMEM_SPEC], [],
        flops, 4_000_000, 14,
    )(place, frames, spare, weight_one)
    (both,) = call(
        grad_kernel, "grad_conv", [pair], [SMEM_SPEC] + [VMEM_SPEC] * 4, [VMEM_SPEC], [],
        flops, 4_000_000, 14,
    )(place, frames, spare, weight_two, pre_act)
    both_mate = swap(both)

    *parts, both = call(
        gradient_kernel, "weight_grads", [rows64] * 3 + [rows32] * 2 + [pair],
        [SMEM_SPEC] + [VMEM_SPEC] * 3 + [ANY_SPEC], [VMEM_SPEC] * 5 + [ANY_SPEC],
        [pltpu.VMEM((2, CH, ROWS), BF16), pltpu.VMEM((27, CH, CH), BF16)],
        2 * flops, 10_000_000, 18, {4: 5},
    )(place, both, both_mate, frames, both)

    def rounds(arrays, axis):
        return [arrays[0]] + [ring_send(arrays[d], axis, d) for d in (1, 2, 3)]

    own, to_after, to_before, kept, given = parts
    across = kept.astype(F32) + ring_send(given, first, 0, pairing).astype(F32)
    arrived = [
        own,
        ring_send(to_after, first, 1),
        ring_send(to_before, first, 3),
        ring_send(across.astype(BF16), first, 2),
    ]
    quarter = call(
        scatter_kernel, "sum_and_split", [rows16] * 4, [SMEM_SPEC] + [VMEM_SPEC] * 4, [VMEM_SPEC] * 4,
        [], 4_000_000, 4_500_000, 12,
    )(place, *arrived)

    (skins,) = call(
        pack_both_kernel, "pack_both", [skin], [VMEM_SPEC, ANY_SPEC], [VMEM_SPEC], [], 1000, 1_000_000, 8,
    )(both, quarter[0])
    before, after = sent_halo(skins)
    mate_before, mate_after = swap(before), swap(after)
    skins_mate = packed_mate(both_mate)
    def added(arrays):
        wide = [array.astype(F32) for array in arrays]
        return (wide[0] + wide[2]) + (wide[1] + wide[3])

    small = added(rounds(quarter, second)).astype(BF16)
    scale = float(128 * ROWS) ** (-0.5)
    whole = (scale * added(rounds([small] * 4, third))).astype(BF16)

    wide, again, half, both = call(
        gather_kernel, "gather_rows", [rows64] * 2 + [rows32, pair],
        [SMEM_SPEC] + [VMEM_SPEC] * 4 + [ANY_SPEC], [VMEM_SPEC] * 3 + [ANY_SPEC], [],
        1000, 2_700_000, 12, {5: 3},
    )(place, *rounds([whole] * 4, second), both)
    half = ring_send(half, first, 2)
    other_half = ring_send(half, first, 0, pairing)
    from_before, from_after = ring_send(wide, first, 1), ring_send(wide, first, 3)
    frame_hidden, frame_grad = call(
        outer_frames_kernel, "outer_frames", [(FRAME_ROWS, TAPS)] * 2, [SMEM_SPEC] + [ANY_SPEC] * 9,
        [VMEM_SPEC] * 2, [full, packed, sems], 1_000_000, 8_000_000, 14,
    )(picks, both, both_mate, skins, before, after, skins_mate, mate_before, mate_after, both)
    output, again = call(
        output_kernel, "output_conv", [(1, ROWS, CH), rows64], [VMEM_SPEC] * 2 + [ANY_SPEC],
        [VMEM_SPEC, ANY_SPEC], [], flops, 4_000_000, 14, {2: 1},
    )(frame_hidden, weight_two, again)
    grad_input, again = call(
        grad_input_kernel, "grad_input_conv", [(1, ROWS, CH), rows64], [VMEM_SPEC] * 2 + [ANY_SPEC],
        [VMEM_SPEC, ANY_SPEC], [], flops, 4_000_000, 14, {2: 1},
    )(frame_grad, weight_one, again)
    early = [(0, 0), (2, 0)]
    late = [(3, 0), (1, 0), (2, 1)]
    grad_one, grad_two = call(
        partial(place_kernel, early), "place_early", [(27, CH, CH)] * 2,
        [SMEM_SPEC] + [VMEM_SPEC] * 4, [ANY_SPEC] * 2,
        [pltpu.SemaphoreType.DMA((2, 2))], 1000, 5_000_000, 12,
    )(place, wide, half, swap(again), swap(half))
    chunks = [from_before, from_after, other_half]
    grad_one, grad_two = call(
        partial(place_kernel, late), "place_late", [(27, CH, CH)] * 2,
        [SMEM_SPEC] + [VMEM_SPEC] * 6 + [ANY_SPEC] * 2, [ANY_SPEC] * 2,
        [pltpu.SemaphoreType.DMA((2, 3))], 1000, 9_000_000, 12, {7: 0, 8: 1},
    )(place, *chunks, *[swap(chunk) for chunk in chunks], grad_one, grad_two)
    return output, grad_input, grad_one, grad_two


def solution(mesh):
    by_brick = P(AXES, None, None)
    in_specs = (by_brick, by_brick, P(), P(), P(AXES), P(AXES, None), P(AXES, None))
    out_specs = (by_brick, by_brick, P(), P())
    return jax.shard_map(
        on_device, mesh=mesh, in_specs=in_specs, out_specs=out_specs, check_vma=False
    )
```

```python
from functools import partial

import jax
import jax.numpy as jnp
from jax import lax
from jax.experimental import pallas as pl
from jax.experimental.pallas import tpu as pltpu
from jax.sharding import PartitionSpec as P

AXES = ("region", "shard")
SIDES = (4, 4, 4, 2)
ROWS = 512
OUTER = 320
CH = 256
TAPS = 2304
FRAME_ROWS = 640
EVEN = (1, 0, 3, 2)
ODD = (3, 2, 1, 0)
F32 = jnp.float32
BF16 = jnp.bfloat16
VMEM_SPEC = pl.BlockSpec(memory_space=pltpu.VMEM)
SMEM_SPEC = pl.BlockSpec(memory_space=pltpu.SMEM)
ANY_SPEC = pl.BlockSpec(memory_space=pl.ANY)
HBM_SPEC = pl.BlockSpec(memory_space=pltpu.HBM)


def coordinates(index):
    return {"x": index // 32, "z": (index // 8) % 4, "y": (index // 2) % 4, "core": index % 2}


def device_at(place):
    return place["x"] * 32 + place["z"] * 8 + place["y"] * 2 + place["core"]


def ring_send(array, axis_of_core, step, pairing=(None, None)):
    pairs = []
    for index in range(128):
        place = coordinates(index)
        axis = axis_of_core[place["core"]]
        place[axis] = (place[axis] + step) % 4
        partner = pairing[place["core"]]
        place["y"] = partner[place["y"]] if partner else place["y"]
        pairs.append((index, device_at(place)))
    return lax.ppermute(array, AXES, pairs)


def swap(array):
    return lax.ppermute(array, AXES, [(index, index ^ 1) for index in range(128)])


def shifted(array, by):
    return lax.ppermute(array, AXES, [(i, i + by) for i in range(128) if 0 <= i + by < 128])


def pack(brick, packed, field):
    packed[field, 0:64] = brick[0:64]
    packed[field, 64:128] = brick[448:512]
    for x in range(1, 7):
        slab = brick[64 * x : 64 * x + 64].astype(F32).reshape(8, 8, CH)
        edges = jnp.concatenate([slab[0], slab[7], slab[:, 0, :], slab[:, 7, :]], axis=0)
        packed[field, 96 + 32 * x : 128 + 32 * x] = edges.astype(BF16)


def build(full, packed, field, pick, out, first_row):
    z_of = lax.broadcasted_iota(jnp.int32, (10, 8, CH), 1)
    centre = pick(1, 1, 1) // 3

    def outer(sx, sy, sz, first, count):
        return packed[field, pick(sx, sy, sz), pl.ds(first, count), :].astype(F32)

    def plane(X, columns):
        below, here, above = [
            jnp.concatenate([low[None], mid, high[None]], axis=0) for low, mid, high in columns
        ]
        shifts = (
            pltpu.roll(jnp.where(z_of == 7, below, here), 1, 1),
            here,
            pltpu.roll(jnp.where(z_of == 0, above, here), 7, 1),
        )
        rows = pl.ds(pl.multiple_of(first_row + X * 64, 64), 64)
        for dz, grid in enumerate(shifts):
            even = grid.reshape(80, CH).astype(BF16)
            odd = grid[1:9].reshape(64, CH).astype(BF16)
            out[rows, (0 + dz) * CH : (1 + dz) * CH] = even[0:64]
            out[rows, (3 + dz) * CH : (4 + dz) * CH] = odd
            out[rows, (6 + dz) * CH : (7 + dz) * CH] = even[16:80]

    def inside(xp):
        return full[field, centre, pl.ds(pl.multiple_of(xp * 64, 64), 64), :].astype(F32).reshape(8, 8, CH)

    for X, sx, face in ((0, 0, 64), (1, 1, 0), (8, 1, 64), (9, 2, 0)):
        columns = []
        for sz in range(3):
            if sx == 1 and sz == 1:
                mid = inside(X - 1)
            else:
                mid = outer(sx, 1, sz, face, 64).reshape(8, 8, CH)
            columns.append((outer(sx, 0, sz, face + 48, 16)[8:16], mid, outer(sx, 2, sz, face, 16)[0:8]))
        plane(X, columns)

    @pl.loop(2, 8)
    def _(X):
        first = pl.multiple_of(64 + 32 * X, 32)
        columns = []
        for sz in range(3):
            if sz == 1:
                mid = inside(X - 1)
            else:
                edge = outer(1, 1, sz, first + 16, 16)
                edge = edge[8:16] if sz == 0 else edge[0:8]
                mid = jnp.broadcast_to(edge[:, None, :], (8, 8, CH))
            columns.append((outer(1, 0, sz, first, 16)[8:16], mid, outer(1, 2, sz, first, 16)[0:8]))
        plane(X, columns)


def convolved(frame, weights):
    total = None
    for plane in range(3):
        term = jnp.dot(
            frame[64 * plane : 64 * plane + ROWS, :],
            weights[9 * plane : 9 * plane + 9].reshape(TAPS, CH),
            preferred_element_type=F32,
        )
        total = term if total is None else total + term
    return total


def convolved_turned(frame, weights):
    total = None
    for k in range(27):
        window = frame[64 * (k // 9) : 64 * (k // 9) + ROWS, (k % 9) * CH : (k % 9 + 1) * CH]
        term = lax.dot_general(
            window, weights[26 - k], (((1,), (1,)), ((), ())), preferred_element_type=F32
        )
        total = term if total is None else total + term
    return total


def picker(pick_ref, which):
    return lambda sx, sy, sz: pick_ref[which, 9 * sx + 3 * sy + sz]


def loaded(own, mate, outers, weights, full, packed, held, sems):
    copies = [
        pltpu.make_async_copy(brick, full.at[:, place], sems.at[place])
        for place, brick in enumerate((own, mate))
    ]
    copies += [
        pltpu.make_async_copy(brick, packed.at[:, place], sems.at[2 + place])
        for place, brick in enumerate(outers)
    ]
    loads = [
        pltpu.make_async_copy(weight, held.at[place], sems.at[8 + place])
        for place, weight in enumerate(weights)
    ]
    for copy in copies + loads:
        copy.start()
    full[:, 2] = jnp.zeros((2, ROWS, CH), BF16)
    packed[:, 6] = jnp.zeros((2, OUTER, CH), BF16)
    for copy in copies:
        copy.wait()
    return loads


def order_kernel(passed, waited_for, passed_out):
    pass


def pack_kernel(features, cotangent, out, packed):
    for place, field in enumerate((features, cotangent)):
        out[place] = field[0]
        pack(field.at[0], packed, place)


def pack_both_kernel(both, waited_for, packed):
    for place in range(2):
        pack(both.at[place], packed, place)


def pack_mate_kernel(mate, packed):
    for place in range(2):
        pack(mate.at[place], packed, place)


def frames_kernel(
    pick_ref, place_ref, own, mate, packed_own, before, after, packed_mate, mate_before, mate_after,
    frames, spare, full, packed, sems
):
    outers = (packed_own, before, after, packed_mate, mate_before, mate_after)
    loaded(own, mate, outers, (), full, packed, None, sems)
    core = place_ref[0]
    build(full, packed, 1 - core, picker(pick_ref, 0), frames, 0)
    build(full, packed, core, picker(pick_ref, 0), spare, 0)
    build(full, packed, 1 - core, picker(pick_ref, 1), frames, FRAME_ROWS)


def hidden_kernel(place_ref, frames, spare, weight_one, pre_act):
    @pl.when(place_ref[0] == 0)
    def _():
        pre_act[...] = convolved(spare, weight_one)

    @pl.when(place_ref[0] != 0)
    def _():
        pre_act[...] = convolved(frames, weight_one)


def grad_kernel(place_ref, frames, spare, weight_two, pre_act_ref, both):
    def finish(frame):
        grad_hidden = convolved_turned(frame, weight_two)
        pre_act = pre_act_ref[...]
        sig = 1.0 / (1.0 + jnp.exp(-pre_act))
        both[0] = (pre_act / (1.0 + jnp.exp(-pre_act))).astype(BF16)
        both[1] = (grad_hidden * sig * (1.0 + pre_act * (1.0 - sig))).astype(BF16)

    @pl.when(place_ref[0] == 0)
    def _():
        finish(frames)

    @pl.when(place_ref[0] != 0)
    def _():
        finish(spare)


def outer_frames_kernel(
    pick_ref, own, mate, packed_own, before, after, packed_mate, mate_before, mate_after, waited_for,
    frame_hidden, frame_grad, full, packed, sems
):
    outers = (packed_own, before, after, packed_mate, mate_before, mate_after)
    loaded(own, mate, outers, (), full, packed, None, sems)
    build(full, packed, 0, picker(pick_ref, 0), frame_hidden, 0)
    build(full, packed, 1, picker(pick_ref, 0), frame_grad, 0)


def output_kernel(frame, weight_two, passed, output, passed_out):
    output[0] = convolved(frame, weight_two).astype(BF16)


def grad_input_kernel(frame, weight_one, passed, grad_input, passed_out):
    grad_input[0] = convolved_turned(frame, weight_one).astype(BF16)


def gradient_kernel(place_ref, both, both_mate, frames, passed, *rest):
    parts, (turned, blocks) = rest[0:5], rest[6:]
    core = place_ref[0]
    turned[0] = both[core].T
    turned[1] = both_mate[core].T

    def run(core):
        for plane in range(3):
            for third in range(3):
                lanes = slice(third * 3 * CH, (third + 1) * 3 * CH)
                row = 64 * plane
                total = jnp.dot(turned[0], frames[row : row + ROWS, lanes], preferred_element_type=F32)
                row += FRAME_ROWS
                total += jnp.dot(turned[1], frames[row : row + ROWS, lanes], preferred_element_type=F32)
                for tap in range(3):
                    k = 9 * plane + 3 * third + tap
                    block = total[:, tap * CH : (tap + 1) * CH].astype(BF16)
                    if core == 0:
                        blocks[26 - k] = block
                    else:
                        blocks[k] = block.T

    @pl.when(core == 0)
    def _():
        run(0)

    @pl.when(core != 0)
    def _():
        run(1)

    for step, part in zip((0, 1, 3), parts[0:3]):
        part[...] = blocks[:, whole_rows(place_ref[1] + step), :]
    for other, part in enumerate(parts[3:5]):
        part[...] = blocks[:, half_rows(place_ref[1] + 2, place_ref[4] + other), :]


def whole_rows(along):
    return pl.ds(pl.multiple_of((along % 4) * 64, 64), 64)


def half_rows(along, bit):
    return pl.ds(pl.multiple_of((along % 4) * 64 + (bit % 2) * 32, 32), 32)


def scatter_kernel(place_ref, own, after, before, across, *outs):
    for step in range(4):
        quarter = (place_ref[3] + step) % 4
        rows = pl.ds(pl.multiple_of(quarter * 16, 16), 16)
        half = pl.ds(pl.multiple_of((quarter % 2) * 16, 16), 16)
        total = own[:, rows, :].astype(F32) + after[:, rows, :].astype(F32) + before[:, rows, :].astype(F32)
        two_on = across[:, half, :].astype(F32)
        total += jnp.where(quarter // 2 == place_ref[4], two_on, jnp.zeros_like(two_on))
        outs[step][...] = total.astype(BF16)


def gather_kernel(place_ref, part0, part1, part2, part3, passed, wide, again, half, passed_out):
    for step, part in enumerate((part0, part1, part2, part3)):
        quarter = (place_ref[3] + 4 - step) % 4
        rows = pl.ds(pl.multiple_of(quarter * 16, 16), 16)
        wide[:, rows, :] = part[...]
        again[:, rows, :] = part[...]

        @pl.when(quarter // 2 == place_ref[4])
        def _(part=part, quarter=quarter):
            half[:, pl.ds(pl.multiple_of((quarter % 2) * 16, 16), 16), :] = part[...]


def place_kernel(hows, place_ref, *refs):
    count = len(hows)
    own, mate = refs[0:count], refs[count : 2 * count]
    grad_one, grad_two, sems = refs[-3:]

    def run(own_dst, mate_dst):
        made = []
        for n, (how, other) in enumerate(hows):
            for side, (dst, part) in enumerate(((own_dst, own[n]), (mate_dst, mate[n]))):
                along, bit = place_ref[1 + side], place_ref[4 + side]
                rows = whole_rows(along + how) if how != 2 else half_rows(along + 2, bit + other)
                made.append(pltpu.make_async_copy(part, dst.at[:, rows, :], sems.at[side, n]))
        for copy in made:
            copy.start()
        for copy in made:
            copy.wait()

    @pl.when(place_ref[0] == 0)
    def _():
        run(grad_two, grad_one)

    @pl.when(place_ref[0] != 0)
    def _():
        run(grad_one, grad_two)


def call(kernel, name, outs, in_specs, out_specs, scratch, flops, moved, mib, aliases=None):
    return pl.pallas_call(
        kernel,
        name=name,
        out_shape=[
            jax.ShapeDtypeStruct(*out) if isinstance(out[0], tuple) else jax.ShapeDtypeStruct(out, BF16)
            for out in outs
        ],
        in_specs=in_specs,
        out_specs=out_specs,
        scratch_shapes=scratch,
        input_output_aliases=aliases or {},
        compiler_params=pltpu.CompilerParams(vmem_limit_bytes=mib * 1024 * 1024),
        cost_estimate=pl.CostEstimate(flops=flops, bytes_accessed=moved, transcendentals=0),
    )


def on_device(
    features, cotangent, weight_one, weight_two, occupancy, neighbour_owner, neighbour_slot
):
    index = lax.axis_index(AXES)
    here = coordinates(index)
    core = here["core"]
    first, second, third = ("x", "z"), ("z", "y"), ("y", "x")

    def along(axis, which):
        return jnp.where(which == 0, here[axis[0]], here[axis[1]])

    bits = jnp.stack([here["y"] % 2, here["y"] // 2])
    pairing = (EVEN, ODD)
    place = jnp.stack(
        [core, along(first, core), along(first, 1 - core), along(second, core), bits[core], bits[1 - core]]
    )
    place = place.astype(jnp.int32)

    graph = jnp.concatenate([occupancy.reshape(1, 1), neighbour_owner], axis=1)
    graph_mate = swap(graph)
    two = jnp.concatenate([graph, graph_mate], axis=0)
    first_brick = index - core - 2
    own_brick = jnp.stack([index, index ^ 1])[:, None]
    own_brick = jnp.where(two[:, 0:1] > 0, own_brick, -1)
    owners = jnp.concatenate([two[:, 1:14], own_brick, two[:, 14:27]], axis=1)
    rel = owners - first_brick
    same = (rel % 2) == core
    kind = jnp.where(rel // 2 == 1, 0, jnp.where(rel // 2 == 0, 1, 2))
    picks = jnp.where(owners >= 0, jnp.where(same, kind, kind + 3), 6).astype(jnp.int32)

    def sent_halo(field):
        return shifted(field, 2), shifted(field, -2)

    flops = 2 * ROWS * TAPS * 3 * CH
    full = pltpu.VMEM((2, 3, ROWS, CH), BF16)
    packed = pltpu.VMEM((2, 7, OUTER, CH), BF16)
    frame = pltpu.VMEM((FRAME_ROWS, TAPS), BF16)
    held = pltpu.VMEM((2, 27, CH, CH), BF16)
    sems = pltpu.SemaphoreType.DMA((10,))
    pair, skin = (2, ROWS, CH), (2, OUTER, CH)
    rows64, rows32, rows16 = (27, 64, CH), (27, 32, CH), (27, 16, CH)

    fields, skins = call(
        pack_kernel, "pack_fields", [pair, skin], [VMEM_SPEC] * 2, [VMEM_SPEC] * 2, [], 1000, 1_000_000, 8,
    )(features, cotangent)
    before, after = sent_halo(skins)

    def packed_mate(mate):
        return call(
            pack_mate_kernel, "pack_mate", [skin], [VMEM_SPEC], [VMEM_SPEC], [], 1000, 1_000_000, 8
        )(mate)[0]

    mate = swap(fields)
    frames, spare = call(
        frames_kernel, "build_frames", [(2 * FRAME_ROWS, TAPS), (FRAME_ROWS, TAPS)],
        [SMEM_SPEC] * 2 + [ANY_SPEC] * 8, [VMEM_SPEC] * 2, [full, packed, sems], 1_000_000, 12_000_000, 14,
    )(picks, place, fields, mate, skins, before, after, packed_mate(mate), swap(before), swap(after))
    (pre_act,) = call(
        hidden_kernel, "first_conv", [((ROWS, CH), F32)], [SMEM_SPEC] + [VMEM_SPEC] * 3, [VMEM_SPEC], [],
        flops, 4_000_000, 14,
    )(place, frames, spare, weight_one)
    (both,) = call(
        grad_kernel, "grad_conv", [pair], [SMEM_SPEC] + [VMEM_SPEC] * 4, [VMEM_SPEC], [],
        flops, 4_000_000, 14,
    )(place, frames, spare, weight_two, pre_act)
    both_mate = swap(both)

    *parts, both = call(
        gradient_kernel, "weight_grads", [rows64] * 3 + [rows32] * 2 + [pair],
        [SMEM_SPEC] + [VMEM_SPEC] * 3 + [ANY_SPEC], [VMEM_SPEC] * 5 + [ANY_SPEC],
        [pltpu.VMEM((2, CH, ROWS), BF16), pltpu.VMEM((27, CH, CH), BF16)],
        2 * flops, 10_000_000, 18, {4: 5},
    )(place, both, both_mate, frames, both)

    def rounds(arrays, axis):
        return [arrays[0]] + [ring_send(arrays[d], axis, d) for d in (1, 2, 3)]

    own, to_after, to_before, kept, given = parts
    across = kept.astype(F32) + ring_send(given, first, 0, pairing).astype(F32)
    arrived = [
        own,
        ring_send(to_after, first, 1),
        ring_send(to_before, first, 3),
        ring_send(across.astype(BF16), first, 2),
    ]
    quarter = call(
        scatter_kernel, "sum_and_split", [rows16] * 4, [SMEM_SPEC] + [VMEM_SPEC] * 4, [VMEM_SPEC] * 4,
        [], 4_000_000, 4_500_000, 12,
    )(place, *arrived)

    (skins,) = call(
        pack_both_kernel, "pack_both", [skin], [VMEM_SPEC, ANY_SPEC], [VMEM_SPEC], [], 1000, 1_000_000, 8,
    )(both, quarter[0])
    before, after = sent_halo(skins)
    mate_before, mate_after = swap(before), swap(after)
    skins_mate = packed_mate(both_mate)
    def added(arrays):
        wide = [array.astype(F32) for array in arrays]
        return (wide[0] + wide[2]) + (wide[1] + wide[3])

    small = added(rounds(quarter, second)).astype(BF16)
    scale = float(128 * ROWS) ** (-0.5)
    whole = (scale * added(rounds([small] * 4, third))).astype(BF16)

    wide, again, half, both = call(
        gather_kernel, "gather_rows", [rows64] * 2 + [rows32, pair],
        [SMEM_SPEC] + [VMEM_SPEC] * 4 + [ANY_SPEC], [VMEM_SPEC] * 3 + [ANY_SPEC], [],
        1000, 2_700_000, 12, {5: 3},
    )(place, *rounds([whole] * 4, second), both)
    half = ring_send(half, first, 2)
    other_half = ring_send(half, first, 0, pairing)
    from_before, from_after = ring_send(wide, first, 1), ring_send(wide, first, 3)
    frame_hidden, frame_grad = call(
        outer_frames_kernel, "outer_frames", [(FRAME_ROWS, TAPS)] * 2, [SMEM_SPEC] + [ANY_SPEC] * 9,
        [VMEM_SPEC] * 2, [full, packed, sems], 1_000_000, 8_000_000, 14,
    )(picks, both, both_mate, skins, before, after, skins_mate, mate_before, mate_after, both)
    output, again = call(
        output_kernel, "output_conv", [(1, ROWS, CH), rows64], [VMEM_SPEC] * 2 + [ANY_SPEC],
        [VMEM_SPEC, ANY_SPEC], [], flops, 4_000_000, 14, {2: 1},
    )(frame_hidden, weight_two, again)
    grad_input, again = call(
        grad_input_kernel, "grad_input_conv", [(1, ROWS, CH), rows64], [VMEM_SPEC] * 2 + [ANY_SPEC],
        [VMEM_SPEC, ANY_SPEC], [], flops, 4_000_000, 14, {2: 1},
    )(frame_grad, weight_one, again)
    hows = [(0, 0), (2, 0), (3, 0), (1, 0), (2, 1)]
    mates = [swap(again), swap(half)]
    grad_one, grad_two = call(
        partial(place_kernel, []), "place_early", [(27, CH, CH)] * 2,
        [SMEM_SPEC] + [VMEM_SPEC] * 4, [ANY_SPEC] * 2,
        [pltpu.SemaphoreType.DMA((2, 2))], 1000, 5_000_000, 12,
    )(place, wide, half, *mates)
    chunks = [from_before, from_after, other_half]
    mates += [swap(chunk) for chunk in chunks]
    grad_one, grad_two = call(
        partial(place_kernel, hows), "place_late", [(27, CH, CH)] * 2,
        [SMEM_SPEC] + [VMEM_SPEC] * 10 + [ANY_SPEC] * 2, [ANY_SPEC] * 2,
        [pltpu.SemaphoreType.DMA((2, 5))], 1000, 14_000_000, 16, {11: 0, 12: 1},
    )(place, wide, half, *chunks, *mates, grad_one, grad_two)
    return output, grad_input, grad_one, grad_two


def solution(mesh):
    by_brick = P(AXES, None, None)
    in_specs = (by_brick, by_brick, P(), P(), P(AXES), P(AXES, None), P(AXES, None))
    out_specs = (by_brick, by_brick, P(), P())
    return jax.shard_map(
        on_device, mesh=mesh, in_specs=in_specs, out_specs=out_specs, check_vma=False
    )
```
